32 devices in a mesh: seq: 8 (over z, y), fsdp: 4 (over x, core).
Axes of the slice: x: 2, y: 2, z: 4, core: 2. Of those that a mesh axis runs over, the one named last changes fastest.
Arguments:
- tokens: bfloat16 [8192, 4096], P('seq', 'fsdp'), may hold values from -6 to 6
- projection: bfloat16 [3, 4096, 2048], P(None, 'seq', 'fsdp'), may hold values from -0.09375 to 0.09375
- log_decay: float32 [8192, 16], P('seq', 'fsdp'), may hold values from -2 to 0, as said below
Outputs:
- attended: bfloat16 [8192, 2048], P('seq', 'fsdp')
The draws below stay inside these ranges and needn't reach their ends.
Inputs may be any that keep to these rules, and one draw needn't show every extreme that they name: `log_decay`: negative logarithms of decay factors, one for each position and head.
All inputs are finite; a program needn't handle non-finite values.
Results may differ from the reference program's by a relative error of at most 0.006.
Values may be sent and summed in bfloat16 or wider, within the bound.
A program may use at most 64 MiB of HBM per device.

```python
import math
import jax
import jax.numpy as jnp
from jax import lax

D = 4096
ATTENDING_GROUPS = 16
HEAD = 128
BLK = 512
TOK_DEV = 1024
TOKENS = 8192


def draw_log_decay(key, part):
    key = jax.random.fold_in(key, 11)
    lookup_vectors = jax.random.split(key, 9)
    fast_count = max(1, ATTENDING_GROUPS // 5)
    medium_count = max(1, ATTENDING_GROUPS // 2 - fast_count)
    offset_scaling = jnp.exp(jnp.clip(jax.random.normal(lookup_vectors[3], (TOKENS, ATTENDING_GROUPS), jnp.float32) * 0.35, -math.log(2.0), math.log(2.0)))
    ranks = jax.random.permutation(lookup_vectors[0], ATTENDING_GROUPS)
    fast = ranks < fast_count
    medium = (ranks >= fast_count) & (ranks < fast_count + medium_count)
    slow_rate = jnp.exp(jax.random.uniform(lookup_vectors[1], (ATTENDING_GROUPS,), jnp.float32, math.log(0.3), math.log(0.9))) / TOKENS
    medium_rate = jnp.exp(jax.random.uniform(lookup_vectors[7], (ATTENDING_GROUPS,), jnp.float32, math.log(0.25), math.log(4.0))) / TOK_DEV
    fast_rate = jnp.exp(jax.random.uniform(lookup_vectors[2], (ATTENDING_GROUPS,), jnp.float32, math.log(1.0 / 50.0), math.log(1.0 / 30.0)))
    default_fading_speed = jnp.where(fast, fast_rate, jnp.where(medium, medium_rate, slow_rate))
    segment_len = max(TOKENS // 64, 1)
    segment_factor = jnp.exp(jax.random.uniform(lookup_vectors[4], (64 + 1, ATTENDING_GROUPS), jnp.float32, -math.log(2.0), math.log(2.0)))
    segment_index = jnp.minimum(jnp.arange(TOKENS) // segment_len, 64)
    stretch_speeds = segment_factor[segment_index]
    leading_spot = jax.random.randint(lookup_vectors[5], (ATTENDING_GROUPS,), 0, TOKENS)
    trailing_spot = (leading_spot + jax.random.randint(lookup_vectors[8], (ATTENDING_GROUPS,), 1, TOKENS)) % TOKENS
    spike_offsets = jnp.stack([leading_spot, trailing_spot])
    spike_strength = jax.random.uniform(lookup_vectors[6], (2, ATTENDING_GROUPS), jnp.float32, 0.6, 0.8)
    sequence_offsets = jnp.arange(TOKENS)[:, None, None]
    sudden_spike_list = jnp.sum(jnp.where(sequence_offsets == spike_offsets[None], jnp.log(spike_strength)[None], 0.0), axis=1)
    return (-default_fading_speed[None, :] * offset_scaling * stretch_speeds + sudden_spike_list).astype(jnp.float32)


def block_levels(stream_key, extent, pieces, low, high):
    loudness, own = 1.0, jax.random.fold_in(stream_key, 6)
    for axis_at, parts in pieces:
        steps = jnp.exp(jax.random.uniform(jax.random.fold_in(own, axis_at), (parts,), jnp.float32, low / len(pieces), high / len(pieces)))
        loudness = loudness * jnp.repeat(steps, extent[axis_at] // parts).reshape([-1 if axis == axis_at else 1 for axis in range(len(extent))])
    return loudness


def scatter_about(rng, extent, deviation, limit, cuts=(), dtype=jnp.bfloat16):
    level = block_levels(rng, extent, cuts, -0.22, 0.18) if cuts else 1.0
    entries = jax.random.normal(rng, extent, jnp.float32) * deviation * level
    return jnp.minimum(jnp.maximum(entries, -limit), limit).astype(dtype)


def setup_inputs(seed: int = 0) -> dict:
    splits = jax.random.split(jax.random.key(seed), 4)
    return {
        "tokens": scatter_about(splits[0], (TOKENS, D), 1.0, 6.0, ((0, 8), (1, 4))),
        "projection": scatter_about(splits[1], (3, D, ATTENDING_GROUPS * HEAD), D ** -0.5, 0.09375, ((1, 8), (2, 4))),
        "log_decay": draw_log_decay(jax.random.fold_in(splits[3], 71), 0),
    }


def block_attention(state, inputs):
    queries, key_vecs, value_vecs, decay = inputs
    running = jnp.cumsum(decay, axis=0)
    across = running.T
    gap = across[:, :, None] - across[:, None, :]
    lower = jnp.arange(gap.shape[1])[:, None] >= jnp.arange(gap.shape[2])[None, :]
    fading = jnp.exp(jnp.where(lower[None], gap, -1e+30))
    scores = jnp.einsum('thd,shd->hts', queries.astype(jnp.float32), key_vecs.astype(jnp.float32), precision=lax.Precision.HIGHEST)
    weights = (fading * scores).astype(jnp.bfloat16)
    intra = jnp.einsum('hts,she->the', weights.astype(jnp.float32), value_vecs.astype(jnp.float32), precision=lax.Precision.HIGHEST)
    inter = jnp.exp(running)[:, :, None] * jnp.einsum('thd,hde->the', queries.astype(jnp.float32), state, precision=lax.Precision.HIGHEST)
    last = running[-1]
    carried = key_vecs.astype(jnp.float32) * jnp.exp(last[None, :] - running)[:, :, None]
    fresh = jnp.einsum('shd,she->hde', carried, value_vecs.astype(jnp.float32), precision=lax.Precision.HIGHEST)
    new_state = jnp.exp(last)[:, None, None] * state + fresh
    mixed = intra + inter
    normed = mixed * lax.rsqrt(lax.optimization_barrier(jnp.mean(mixed * mixed, axis=-1, keepdims=True)) + 1e-06)
    return (new_state, normed.astype(jnp.bfloat16))

def reference(tokens, projection, log_decay):
    block_count = TOKENS // BLK
    query_raw = jnp.dot(tokens, projection[0], preferred_element_type=jnp.float32)
    key_raw = jnp.dot(tokens, projection[1], preferred_element_type=jnp.float32)
    value_raw = jnp.dot(tokens, projection[2], preferred_element_type=jnp.float32)
    queries = jax.nn.silu(query_raw).astype(jnp.bfloat16).reshape(block_count, BLK, ATTENDING_GROUPS, HEAD)
    key_vecs = jax.nn.silu(key_raw).astype(jnp.bfloat16).reshape(block_count, BLK, ATTENDING_GROUPS, HEAD)
    value_vecs = value_raw.astype(jnp.bfloat16).reshape(block_count, BLK, ATTENDING_GROUPS, HEAD)
    decay = log_decay.reshape(block_count, BLK, ATTENDING_GROUPS)
    start = jnp.zeros((ATTENDING_GROUPS, HEAD, HEAD), jnp.float32)
    final, outputs = lax.scan(block_attention, start, (queries, key_vecs, value_vecs, decay))
    return outputs.reshape(TOKENS, ATTENDING_GROUPS * HEAD)
```

```python
import functools

import jax
import jax.numpy as jnp
from jax import lax
from jax.experimental import pallas as pl
from jax.experimental.pallas import tpu as pltpu
from jax.sharding import PartitionSpec as P

BLK = 512
HEAD = 128
PIECES = 4
MESH = pl.DeviceIdType.MESH
X, Y, D, C, CX, CY, CD = range(7)
F32 = jnp.float32
BF16 = jnp.bfloat16


def silu(v):
    return v / (1.0 + jnp.exp(-v))


def dot(a, b, dims=((1,), (0,))):
    return lax.dot_general(a, b, (dims, ((), ())), preferred_element_type=F32)


def split(v):
    high = v.astype(BF16)
    return high, (v - high.astype(F32)).astype(BF16)


def kernel(
    S,
    Fn,
    tok_in,
    proj_in,
    dec_in,
    out,
    tok,
    wts,
    dec,
    cols,
    fade,
    keys,
    vals,
    qry,
    before,
    own_state,
    s_in,
    s_out,
    done,
    tsend,
    trecv,
    wloc,
    wysend,
    wyrecv,
    wrsend,
    wlsend,
    wrecv,
    misc,
    osend,
    orecv,
    oloc,
):
    Z = S // 2
    s, f = lax.axis_index("seq"), lax.axis_index("fsdp")
    z, y = s // 2, s % 2
    x, c = f // 2, f % 2
    rows, kf = tok_in.shape
    ks = proj_in.shape[1]
    half = proj_in.shape[2] // 2
    heads = half // HEAD
    nb = rows // BLK
    depth = 2 * ks
    prow = rows // PIECES

    to_x = (s, (1 - x) * 2 + c)
    to_y = (z * 2 + 1 - y, f)
    to_c = (s, x * 2 + 1 - c)
    to_r = (jnp.minimum(z + 1, Z - 1) * 2 + y, f)
    to_l = (jnp.maximum(z - 1, 0) * 2 + y, f)
    has_l, has_r = z > 0, z < Z - 1

    def shard(yy, xx, cc):
        return yy * Fn + xx * 2 + cc

    place = {
        X: shard(y, 1 - x, c),
        Y: shard(1 - y, x, c),
        D: shard(1 - y, 1 - x, c),
        C: shard(y, x, 1 - c),
        CX: shard(y, 1 - x, 1 - c),
        CY: shard(1 - y, x, 1 - c),
        CD: shard(1 - y, 1 - x, 1 - c),
    }
    mine = shard(y, x, c)

    def remote(src, dst, ssem, rsem, to):
        return pltpu.make_async_remote_copy(
            src_ref=src, dst_ref=dst, send_sem=ssem, recv_sem=rsem, device_id=to, device_id_type=MESH
        )

    barrier = pltpu.get_barrier_semaphore()
    for to in (to_x, to_y, to_c):
        pl.semaphore_signal(barrier, inc=1, device_id=to, device_id_type=MESH)

    @pl.when(has_l)
    def _():
        pl.semaphore_signal(barrier, inc=1, device_id=to_l, device_id_type=MESH)

    @pl.when(has_r)
    def _():
        pl.semaphore_signal(barrier, inc=1, device_id=to_r, device_id_type=MESH)

    pl.semaphore_wait(barrier, 3 + (z + Z - 1) // Z + (2 * Z - 2 - z) // Z)

    def tcopy(kind, i, to, at, src=None):
        here = tok.at[at, pl.ds(i * prow, prow)]
        return remote(here if src is None else src, here, tsend.at[kind, i], trecv.at[kind, i], to)

    def own_tok(kind, i, to):
        return tcopy(kind, i, to, mine, tok_in.at[pl.ds(i * prow, prow)])

    def got_tok(kind, i):
        tcopy(kind, i, to_c, place[kind]).wait_recv()

    def via_y(i):
        return i == PIECES - 1

    def tok_step(i):
        got_tok(X, i)
        tcopy(CX, i, to_c, place[X]).start()
        if via_y(i):
            tcopy(D, i, to_y, place[X]).start()
        got_tok(Y, i)
        tcopy(CY, i, to_c, place[Y]).start()
        if not via_y(i):
            tcopy(D, i, to_x, place[Y]).start()

    def diag_step(i):
        got_tok(D, i)
        tcopy(CD, i, to_c, place[D]).start()

    parts = [(1, 0, half), (2, 0, half)]
    for h in range(heads):
        parts.append((0, h * HEAD, HEAD))

    def wslot(n, at):
        p, lo, width = parts[n]
        return wts.at[p, at, :, :, pl.ds(lo, width)]

    def wmember(n, yy):
        p, lo, width = parts[n]
        return wts.at[p, z, yy, :, pl.ds(lo, width)]

    def wsource(n, yy):
        p, lo, width = parts[n]
        return proj_in.at[p, :, pl.ds(pl.multiple_of(yy * half + lo, HEAD), width)]

    def wlocal(n):
        return pltpu.make_async_copy(wsource(n, y), wmember(n, y), wloc.at[n])

    def wpair(n):
        return remote(wsource(n, 1 - y), wmember(n, y), wysend.at[n], wyrecv.at[n], to_y)

    def wright(n, at):
        slot = wslot(n, at)
        return remote(slot, slot, wrsend.at[n, at], wrecv.at[n, at], to_r)

    def wleft(n, at):
        slot = wslot(n, at)
        return remote(slot, slot, wlsend.at[n, at], wrecv.at[n, at], to_l)

    def own_part(n):
        wlocal(n).wait()
        remote(wsource(n, y), wmember(n, 1 - y), wysend.at[n], wyrecv.at[n], to_y).wait_recv()

        @pl.when(has_r)
        def _():
            wright(n, z).start()

        @pl.when(has_l)
        def _():
            wleft(n, z).start()

    def wstep(n, d):
        @pl.when(z - d >= 0)
        def _():
            wright(n, z - d).wait_recv()

            @pl.when(has_r)
            def _():
                wright(n, z - d).start()

        @pl.when(z + d <= Z - 1)
        def _():
            wleft(n, z + d).wait_recv()

            @pl.when(has_l)
            def _():
                wleft(n, z + d).start()

    dec_copy = remote(dec_in.at[1 - y], dec.at[y], misc.at[0], misc.at[1], to_y)
    dec_copy.start()
    dec_local = pltpu.make_async_copy(dec_in.at[y], dec.at[y], misc.at[2])
    for n in (0, 1):
        wpair(n).start()
    for n in range(len(parts)):
        wlocal(n).start()
    for i in range(PIECES):
        own_tok(X, i, to_x).start()
        own_tok(Y, i, to_y).start()
        own_tok(C, i, to_c).start()
    for n in range(2, len(parts)):
        wpair(n).start()
    tok_local = pltpu.make_async_copy(tok_in, tok.at[mine], misc.at[3])
    tok_local.start()
    own_part(0)
    own_part(1)

    dec_local.start()
    dec_local.wait()
    remote(dec_in.at[y], dec.at[1 - y], misc.at[0], misc.at[1], to_y).wait_recv()
    lane = lax.broadcasted_iota(jnp.int32, (8, BLK), 1)
    for yy in range(2):
        run = dec[yy]
        step = 1
        while step < BLK:
            run = run + jnp.where(lane >= step, pltpu.roll(run, step, 1), 0.0)
            step *= 2
        dec[yy] = run
        cols[yy] = run.T
    for h in range(heads):
        for b in range(nb):
            at = h * nb + b

            def fading(yy, _, h=h, b=b, at=at):
                gap = cols[yy, :, at : at + 1] - dec[yy, at : at + 1, :]
                t = lax.broadcasted_iota(jnp.int32, (BLK, BLK), 0)
                u = lax.broadcasted_iota(jnp.int32, (BLK, BLK), 1)
                fade[h, yy * nb + b] = jnp.exp(jnp.where(t >= u, gap, -1e30))
                return 0

            lax.fori_loop(0, 2, fading, 0)

    def project(n, yy, store):
        p, lo, width = parts[n]

        def tile(i, _):
            r = pl.ds(pl.multiple_of(i * BLK, BLK), BLK)
            total = None
            for at in range(Z):
                ff, off = (at * depth) // kf, (at * depth) % kf
                w = wts[p, at, :, :, lo : lo + width].reshape(depth, width)
                part = dot(tok[yy * Fn + ff, r, off : off + depth], w)
                total = part if total is None else total + part
            store(pl.ds(pl.multiple_of(yy * rows + i * BLK, BLK), BLK), total)
            return 0

        lax.fori_loop(0, nb, tile, 0)

    def store_key(r, v):
        keys[r, :] = silu(v).astype(BF16)

    def store_val(r, v):
        vals[r, :] = v.astype(BF16)

    last = Z - 1
    early = [(0, d) for d in range(1, Z)] + [(1, 1)]
    per = -(-len(early) // PIECES)
    for i in range(PIECES):
        tok_step(i)
        for n, d in early[i * per : (i + 1) * per]:
            wstep(n, d)
    if heads > 0:
        own_part(2)
    for i in range(PIECES):
        got_tok(C, i)
        got_tok(CX, i)
    tok_local.wait()
    project(0, y, store_key)
    middle = [(1, d) for d in range(2, Z)]
    per = -(-len(middle) // 2)
    for i in range(2):
        for j in range(i * PIECES // 2, (i + 1) * PIECES // 2):
            diag_step(j)
        for n, d in middle[i * per : (i + 1) * per]:
            wstep(n, d)
    for n in range(3, len(parts)):
        own_part(n)
    project(1, y, store_val)
    wstep(2, 1)
    for i in range(PIECES):
        got_tok(CY, i)
        got_tok(CD, i)
    project(0, 1 - y, store_key)
    project(1, 1 - y, store_val)

    for h in range(heads):
        hc = slice(h * HEAD, (h + 1) * HEAD)
        state = jnp.zeros((HEAD, HEAD), F32)
        for j in range(2 * nb):
            yy, b = j // nb, j % nb
            at = h * nb + b
            before[h, j] = state
            run = cols[yy, :, at : at + 1]
            end = dec[yy, at : at + 1, BLK - 1 : BLK]
            r = slice(j * BLK, (j + 1) * BLK)
            carried = keys[r, hc].astype(F32) * jnp.exp(end - run)
            high, low = split(carried)
            v = vals[r, hc]
            fresh = dot(high, v, ((0,), (0,))) + dot(low, v, ((0,), (0,)))
            state = jnp.exp(end) * state + fresh
        own_state[h] = state

    for n in range(2, len(parts)):
        for d in range(1, Z):
            if (n, d) != (2, 1) and not (n == len(parts) - 1 and d == last):
                wstep(n, d)

    state_copy = remote(s_out, s_in, misc.at[4], misc.at[5], to_r)

    @pl.when(has_l)
    def _():
        state_copy.wait_recv()

    @pl.when(z == 0)
    def _():
        s_in[...] = jnp.zeros_like(s_in)

    for h in range(heads):
        lead = jnp.zeros((1, 1), F32)
        for j in range(2 * nb):
            yy, b = j // nb, j % nb
            at = h * nb + b
            before[h, j] = before[h, j] + jnp.exp(lead) * s_in[h]
            lead = lead + dec[yy, at : at + 1, BLK - 1 : BLK]
        s_out[h] = own_state[h] + jnp.exp(lead) * s_in[h]

    @pl.when(has_r)
    def _():
        state_copy.start()

    def place_out(h, b, who):
        return out.at[
            pl.ds(b * BLK, BLK), pl.ds(pl.multiple_of(who * half + h * HEAD, HEAD), HEAD)
        ]

    def give(h, b):
        src = done.at[h, (1 - y) * nb + b]
        return remote(src, place_out(h, b, y), osend.at[h, b], orecv.at[h, b], to_y)

    def keep(h, b):
        return pltpu.make_async_copy(done.at[h, y * nb + b], place_out(h, b, y), oloc.at[h, b])

    def attend(h, yy, b):
        at = h * nb + b
        j = yy * nb + b
        hc = slice(h * HEAD, (h + 1) * HEAD)
        r = pl.ds(pl.multiple_of(j * BLK, BLK), BLK)
        q, k, v = qry[r, :], keys[r, hc], vals[r, hc]
        scores = dot(q, k, ((1,), (1,)))
        weights = (fade[h, j] * scores).astype(BF16)
        high, low = split(before[h, j])
        inter = dot(q, jnp.concatenate([high, low], axis=1))
        inter = inter[:, :HEAD] + inter[:, HEAD:]
        mixed = dot(weights, v) + jnp.exp(cols[yy, :, at : at + 1]) * inter
        scale = lax.rsqrt(jnp.mean(mixed * mixed, axis=-1, keepdims=True) + 1e-6)
        done[h, j] = (mixed * scale).astype(BF16)

    def store_query(r, v):
        qry[r, :] = silu(v).astype(BF16)

    for h in range(heads):
        if h == heads - 1:
            wstep(2 + h, last)
        project(2 + h, 1 - y, store_query)
        for b in range(nb):
            attend(h, 1 - y, b)
            give(h, b).start()
        project(2 + h, y, store_query)
        for b in range(nb):
            attend(h, y, b)
            keep(h, b).start()

    for h in range(heads):
        for b in range(nb):
            keep(h, b).wait()
            give(h, b).wait_send()
            remote(
                done.at[h, y * nb + b],
                place_out(h, b, 1 - y),
                osend.at[h, b],
                orecv.at[h, b],
                to_y,
            ).wait_recv()

    @pl.when(has_r)
    def _():
        state_copy.wait_send()

    dec_copy.wait_send()
    for n in range(len(parts)):
        wpair(n).wait_send()
        for at in range(Z):

            @pl.when(has_r & (at <= z))
            def _():
                wright(n, at).wait_send()

            @pl.when(has_l & (at >= z))
            def _():
                wleft(n, at).wait_send()

    for i in range(PIECES):
        own_tok(X, i, to_x).wait_send()
        own_tok(Y, i, to_y).wait_send()
        own_tok(C, i, to_c).wait_send()
        tcopy(CX, i, to_c, place[X]).wait_send()
        tcopy(CY, i, to_c, place[Y]).wait_send()
        tcopy(CD, i, to_c, place[D]).wait_send()
        if via_y(i):
            tcopy(D, i, to_y, place[X]).wait_send()
        else:
            tcopy(D, i, to_x, place[Y]).wait_send()


def on_device(S, Fn, tokens, projection, log_decay):
    rows, kf = tokens.shape
    ks, width = projection.shape[1:]
    Z = S // 2
    half = width // 2
    heads = half // HEAD
    nb = rows // BLK
    parts = 2 + heads
    dec = log_decay.T.reshape(2, heads * nb, BLK)
    dec = jnp.pad(dec, ((0, 0), (0, 8 - heads * nb), (0, 0)))
    dma = pltpu.SemaphoreType.DMA
    any_spec = pl.BlockSpec(memory_space=pl.ANY)
    return pl.pallas_call(
        functools.partial(kernel, S, Fn),
        out_shape=jax.ShapeDtypeStruct((rows, width), BF16),
        in_specs=[any_spec] * 3,
        out_specs=any_spec,
        scratch_shapes=[
            pltpu.VMEM((2 * Fn, rows, kf), BF16),
            pltpu.VMEM((3, Z, 2, ks, half), BF16),
            pltpu.VMEM((2, 8, BLK), F32),
            pltpu.VMEM((2, BLK, 8), F32),
            pltpu.VMEM((heads, 2 * nb, BLK, BLK), F32),
            pltpu.VMEM((2 * rows, half), BF16),
            pltpu.VMEM((2 * rows, half), BF16),
            pltpu.VMEM((2 * rows, HEAD), BF16),
            pltpu.VMEM((heads, 2 * nb, HEAD, HEAD), F32),
            pltpu.VMEM((heads, HEAD, HEAD), F32),
            pltpu.VMEM((heads, HEAD, HEAD), F32),
            pltpu.VMEM((heads, HEAD, HEAD), F32),
            pltpu.VMEM((heads, 2 * nb, BLK, HEAD), BF16),
            dma((7, PIECES)),
            dma((7, PIECES)),
            dma((parts,)),
            dma((parts,)),
            dma((parts,)),
            dma((parts, Z)),
            dma((parts, Z)),
            dma((parts, Z)),
            dma((6,)),
            dma((heads, nb)),
            dma((heads, nb)),
            dma((heads, nb)),
        ],
        compiler_params=pltpu.CompilerParams(
            collective_id=0, has_side_effects=True, vmem_limit_bytes=52 * 1024 * 1024
        ),
    )(tokens, projection, dec)


def solution(mesh):
    S, Fn = mesh.shape["seq"], mesh.shape["fsdp"]
    return jax.shard_map(
        functools.partial(on_device, S, Fn),
        mesh=mesh,
        in_specs=(P("seq", "fsdp"), P(None, "seq", "fsdp"), P("seq", "fsdp")),
        out_specs=P("seq", "fsdp"),
        check_vma=False,
    )
```

```python
import functools

import jax
import jax.numpy as jnp
from jax import lax
from jax.experimental import pallas as pl
from jax.experimental.pallas import tpu as pltpu
from jax.sharding import PartitionSpec as P

BLK = 512
HEAD = 128
PIECES = 4
AHEAD = 2
MESH = pl.DeviceIdType.MESH
X, Y, D, C, CX, CY, CD = range(7)
F32 = jnp.float32
BF16 = jnp.bfloat16


def silu(v):
    return v / (1.0 + jnp.exp(-v))


def dot(a, b, dims=((1,), (0,))):
    return lax.dot_general(a, b, (dims, ((), ())), preferred_element_type=F32)


def split(v):
    high = v.astype(BF16)
    return high, (v - high.astype(F32)).astype(BF16)


def kernel(
    S,
    Fn,
    tok_in,
    proj_in,
    dec_in,
    out,
    tok,
    wts,
    dec,
    cols,
    fade,
    keys,
    vals,
    qacc,
    fresh,
    before,
    s_in,
    s_out,
    done,
    tsend,
    trecv,
    wloc,
    wysend,
    wyrecv,
    wrsend,
    wlsend,
    wrecv,
    misc,
    osend,
    orecv,
    oloc,
):
    Z = S // 2
    s, f = lax.axis_index("seq"), lax.axis_index("fsdp")
    z, y = s // 2, s % 2
    x, c = f // 2, f % 2
    rows, kf = tok_in.shape
    ks = proj_in.shape[1]
    half = proj_in.shape[2] // 2
    heads = half // HEAD
    nb = rows // BLK
    depth = 2 * ks
    prow = rows // PIECES

    to_x = (s, (1 - x) * 2 + c)
    to_y = (z * 2 + 1 - y, f)
    to_c = (s, x * 2 + 1 - c)
    to_r = (jnp.minimum(z + 1, Z - 1) * 2 + y, f)
    to_l = (jnp.maximum(z - 1, 0) * 2 + y, f)
    has_l, has_r = z > 0, z < Z - 1

    def shard(yy, xx, cc):
        return yy * Fn + xx * 2 + cc

    place = {
        X: shard(y, 1 - x, c),
        Y: shard(1 - y, x, c),
        D: shard(1 - y, 1 - x, c),
        C: shard(y, x, 1 - c),
        CX: shard(y, 1 - x, 1 - c),
        CY: shard(1 - y, x, 1 - c),
        CD: shard(1 - y, 1 - x, 1 - c),
    }
    mine = shard(y, x, c)

    def remote(src, dst, ssem, rsem, to):
        return pltpu.make_async_remote_copy(
            src_ref=src, dst_ref=dst, send_sem=ssem, recv_sem=rsem, device_id=to, device_id_type=MESH
        )

    barrier = pltpu.get_barrier_semaphore()
    for to in (to_x, to_y, to_c):
        pl.semaphore_signal(barrier, inc=1, device_id=to, device_id_type=MESH)

    @pl.when(has_l)
    def _():
        pl.semaphore_signal(barrier, inc=1, device_id=to_l, device_id_type=MESH)

    @pl.when(has_r)
    def _():
        pl.semaphore_signal(barrier, inc=1, device_id=to_r, device_id_type=MESH)

    pl.semaphore_wait(barrier, 3 + (z + Z - 1) // Z + (2 * Z - 2 - z) // Z)

    def tcopy(kind, i, to, at, src=None):
        here = tok.at[at, pl.ds(i * prow, prow)]
        return remote(here if src is None else src, here, tsend.at[kind, i], trecv.at[kind, i], to)

    def own_tok(kind, i, to):
        return tcopy(kind, i, to, mine, tok_in.at[pl.ds(i * prow, prow)])

    def got_tok(kind, i):
        tcopy(kind, i, to_c, place[kind]).wait_recv()

    def via_y(i):
        return i == PIECES - 1

    def side_step(i):
        got_tok(X, i)
        tcopy(CX, i, to_c, place[X]).start()
        if via_y(i):
            tcopy(D, i, to_y, place[X]).start()
        if i + AHEAD < PIECES:
            own_tok(X, i + AHEAD, to_x).start()

    def pair_step(i):
        got_tok(Y, i)
        tcopy(CY, i, to_c, place[Y]).start()
        if not via_y(i):
            tcopy(D, i, to_x, place[Y]).start()
        if i + AHEAD < PIECES:
            own_tok(Y, i + AHEAD, to_y).start()

    def diag_step(i):
        got_tok(D, i)
        tcopy(CD, i, to_c, place[D]).start()

    parts = [(1, 0, half), (2, 0, half)]
    for h in range(heads):
        parts.append((0, h * HEAD, HEAD))

    def wslot(n, at):
        p, lo, width = parts[n]
        return wts.at[p, at, :, :, pl.ds(lo, width)]

    def wmember(n, yy):
        p, lo, width = parts[n]
        return wts.at[p, z, yy, :, pl.ds(lo, width)]

    def wsource(n, yy):
        p, lo, width = parts[n]
        return proj_in.at[p, :, pl.ds(pl.multiple_of(yy * half + lo, HEAD), width)]

    def wlocal(n):
        return pltpu.make_async_copy(wsource(n, y), wmember(n, y), wloc.at[n])

    def wpair(n):
        return remote(wsource(n, 1 - y), wmember(n, y), wysend.at[n], wyrecv.at[n], to_y)

    def wright(n, at):
        slot = wslot(n, at)
        return remote(slot, slot, wrsend.at[n, at], wrecv.at[n, at], to_r)

    def wleft(n, at):
        slot = wslot(n, at)
        return remote(slot, slot, wlsend.at[n, at], wrecv.at[n, at], to_l)

    def own_part(n):
        wlocal(n).wait()
        remote(wsource(n, y), wmember(n, 1 - y), wysend.at[n], wyrecv.at[n], to_y).wait_recv()

        @pl.when(has_r)
        def _():
            wright(n, z).start()

        @pl.when(has_l)
        def _():
            wleft(n, z).start()

    def wstep(n, d):
        @pl.when(z - d >= 0)
        def _():
            wright(n, z - d).wait_recv()

            @pl.when(has_r)
            def _():
                wright(n, z - d).start()

        @pl.when(z + d <= Z - 1)
        def _():
            wleft(n, z + d).wait_recv()

            @pl.when(has_l)
            def _():
                wleft(n, z + d).start()

    def wsteps(n, i, slots=3):
        for d in range(1 + i * (Z - 1) // slots, 1 + (i + 1) * (Z - 1) // slots):
            wstep(n, d)

    dec_copy = remote(dec_in.at[1 - y], dec.at[y], misc.at[0], misc.at[1], to_y)
    dec_copy.start()
    dec_local = pltpu.make_async_copy(dec_in.at[y], dec.at[y], misc.at[2])
    for n in (0, 1):
        wpair(n).start()
    for n in range(2):
        wlocal(n).start()
    for i in range(AHEAD):
        own_tok(X, i, to_x).start()
        own_tok(Y, i, to_y).start()
    for i in range(PIECES):
        own_tok(C, i, to_c).start()
    for n in range(2, len(parts)):
        wlocal(n).start()
    tok_local = pltpu.make_async_copy(tok_in, tok.at[mine], misc.at[3])
    tok_local.start()
    own_part(0)
    own_part(1)

    dec_local.start()
    dec_local.wait()
    remote(dec_in.at[y], dec.at[1 - y], misc.at[0], misc.at[1], to_y).wait_recv()
    lane = lax.broadcasted_iota(jnp.int32, (8, BLK), 1)
    for yy in range(2):
        run = dec[yy]
        step = 1
        while step < BLK:
            run = run + jnp.where(lane >= step, pltpu.roll(run, step, 1), 0.0)
            step *= 2
        dec[yy] = run
        cols[yy] = run.T
    for h in range(heads):
        for b in range(nb):
            at = h * nb + b

            def fading(yy, _, h=h, b=b, at=at):
                gap = cols[yy, :, at : at + 1] - dec[yy, at : at + 1, :]
                t = lax.broadcasted_iota(jnp.int32, (BLK, BLK), 0)
                u = lax.broadcasted_iota(jnp.int32, (BLK, BLK), 1)
                fade[h, yy * nb + b] = jnp.exp(jnp.where(t >= u, gap, -1e30))
                return 0

            lax.fori_loop(0, 2, fading, 0)

    def chunk(n, yy, r, at):
        p, lo, width = parts[n]
        w = wts[p, at, :, :, lo : lo + width].reshape(depth, width)
        ff, off = (at * depth) // kf, (at * depth) % kf
        if depth == kf:
            return dot(tok[yy * Fn + ff, r, :], w)
        if not isinstance(at, int):
            off = pl.multiple_of(off, HEAD)
        return dot(tok[yy * Fn + ff, r, pl.ds(off, depth)], w)

    def project(n, yy, i):
        r = pl.ds(i * BLK, BLK)
        total = chunk(n, yy, r, 0)
        for at in range(1, Z):
            total = total + chunk(n, yy, r, at)
        to = pl.ds(pl.multiple_of(yy * rows + i * BLK, BLK), BLK)
        if n == 0:
            keys[to, :] = silu(total).astype(BF16)
        else:
            vals[to, :] = total.astype(BF16)

    def states(yy, b):
        j = yy * nb + b
        r = pl.ds(pl.multiple_of(j * BLK, BLK), BLK)
        for h in range(heads):
            hc = slice(h * HEAD, (h + 1) * HEAD)
            at = h * nb + b
            run = cols[yy, :, at : at + 1]
            end = dec[yy, at : at + 1, BLK - 1 : BLK]
            high, low = split(keys[r, hc].astype(F32) * jnp.exp(end - run))
            v = vals[r, hc]
            fresh[h, j] = dot(high, v, ((0,), (0,))) + dot(low, v, ((0,), (0,)))

    def got_core(kinds, i):
        lo, hi = i * PIECES // nb, (i + 1) * PIECES // nb
        for j in range(lo, hi):
            for kind in kinds:
                got_tok(kind, j)

    near = (z // (Z - 1)) * (Z - 1)
    far = Z - 1 - near

    def begin_query(h):
        def tile(i, _):
            yy, b = i // nb, i % nb
            r = pl.ds(pl.multiple_of(b * BLK, BLK), BLK)
            total = chunk(2 + h, yy, r, near)
            for at in range(1, Z - 1):
                total = total + chunk(2 + h, yy, r, at)
            qacc[h, pl.ds(pl.multiple_of(i * BLK, BLK), BLK), :] = total
            return 0

        lax.fori_loop(0, 2 * nb, tile, 0)

    side_step(0)
    wsteps(0, 0)
    pair_step(0)
    side_step(1)
    wsteps(0, 1)
    pair_step(1)
    for n in range(2, len(parts)):
        wpair(n).start()
    for i in range(2, PIECES):
        side_step(i)
        if i == 2:
            wsteps(0, 2)
            pair_step(2)
    own_part(2)
    wsteps(1, 0)
    tok_local.wait()
    got_core((C, CX), 0)
    project(0, y, 0)
    for i in range(3, PIECES):
        pair_step(i)
    wsteps(1, 1)
    for i in range(1, nb):
        got_core((C, CX), i)
        project(0, y, i)
    diag_step(0)
    wsteps(1, 2)
    for n in range(3, len(parts)):
        own_part(n)
    project(1, y, 0)
    diag_step(PIECES - 1)
    for i in range(1, PIECES // nb):
        diag_step(i)
    for i in range(1, nb):
        project(1, y, i)
    wsteps(2, 0)
    got_core((CY, CD), 0)
    project(0, 1 - y, 0)
    project(1, 1 - y, 0)
    wsteps(2, 1)
    for b in range(nb):
        states(y, b)
    states(1 - y, 0)
    for i in range(PIECES // nb, PIECES - 1):
        diag_step(i)
    for i in range(1, nb):
        got_core((CY, CD), i)
        project(0, 1 - y, i)
        project(1, 1 - y, i)
        states(1 - y, i)

    state_copy = remote(s_out, s_in, misc.at[4], misc.at[5], to_r)

    def chain():
        for h in range(heads):
            state = jnp.zeros((HEAD, HEAD), F32)
            lead = jnp.zeros((1, 1), F32)
            for j in range(2 * nb):
                yy, at = j // nb, h * nb + j % nb
                end = dec[yy, at : at + 1, BLK - 1 : BLK]
                before[h, j] = state
                state = jnp.exp(end) * state + fresh[h, j]
                lead = lead + end
            s_out[h] = state

        @pl.when(has_l)
        def _():
            state_copy.wait_recv()
            for h in range(heads):
                lead = jnp.zeros((1, 1), F32)
                for j in range(2 * nb):
                    yy, at = j // nb, h * nb + j % nb
                    lead = lead + dec[yy, at : at + 1, BLK - 1 : BLK]
                s_out[h] = s_out[h] + jnp.exp(lead) * s_in[h]

        @pl.when(has_r)
        def _():
            state_copy.start()

        @pl.when(has_l)
        def _():
            for h in range(heads):
                lead = jnp.zeros((1, 1), F32)
                for j in range(2 * nb):
                    yy, at = j // nb, h * nb + j % nb
                    before[h, j] = before[h, j] + jnp.exp(lead) * s_in[h]
                    lead = lead + dec[yy, at : at + 1, BLK - 1 : BLK]

    @pl.when(z < Z // 2)
    def _():
        chain()

    wsteps(2, 2)
    begin_query(0)
    for n in range(3, len(parts)):
        for d in range(1, Z - 1):
            wstep(n, d)

    @pl.when(z >= Z // 2)
    def _():
        chain()

    def place_out(h, b, who):
        return out.at[
            pl.ds(b * BLK, BLK), pl.ds(pl.multiple_of(who * half + h * HEAD, HEAD), HEAD)
        ]

    def give(h, b):
        src = done.at[h, (1 - y) * nb + b]
        return remote(src, place_out(h, b, y), osend.at[h, b], orecv.at[h, b], to_y)

    def keep(h, b):
        return pltpu.make_async_copy(done.at[h, y * nb + b], place_out(h, b, y), oloc.at[h, b])

    def attend(h, yy, b):
        at = h * nb + b
        j = yy * nb + b
        hc = slice(h * HEAD, (h + 1) * HEAD)
        r = pl.ds(pl.multiple_of(j * BLK, BLK), BLK)
        total = qacc[h, r, :] + chunk(2 + h, yy, pl.ds(b * BLK, BLK), far)
        q, k, v = silu(total).astype(BF16), keys[r, hc], vals[r, hc]
        scores = dot(q, k, ((1,), (1,)))
        weights = (fade[h, j] * scores).astype(BF16)
        high, low = split(before[h, j])
        inter = dot(q, jnp.concatenate([high, low], axis=1))
        inter = inter[:, :HEAD] + inter[:, HEAD:]
        mixed = dot(weights, v) + jnp.exp(cols[yy, :, at : at + 1]) * inter
        scale = lax.rsqrt(jnp.mean(mixed * mixed, axis=-1, keepdims=True) + 1e-6)
        done[h, j] = (mixed * scale).astype(BF16)

    for h in range(heads):
        if h > 0:
            wstep(2 + h, Z - 1)
        for b in range(nb):
            attend(h, 1 - y, b)
            give(h, b).start()
        if h + 1 < heads:
            begin_query(h + 1)
        for b in range(nb):
            attend(h, y, b)
            keep(h, b).start()

    for h in range(heads):
        for b in range(nb):
            keep(h, b).wait()
            give(h, b).wait_send()
            remote(
                done.at[h, y * nb + b],
                place_out(h, b, 1 - y),
                osend.at[h, b],
                orecv.at[h, b],
                to_y,
            ).wait_recv()

    @pl.when(has_r)
    def _():
        state_copy.wait_send()

    dec_copy.wait_send()
    for n in range(len(parts)):
        wpair(n).wait_send()
        for at in range(Z):

            @pl.when(has_r & (at <= z))
            def _():
                wright(n, at).wait_send()

            @pl.when(has_l & (at >= z))
            def _():
                wleft(n, at).wait_send()

    for i in range(PIECES):
        own_tok(X, i, to_x).wait_send()
        own_tok(Y, i, to_y).wait_send()
        own_tok(C, i, to_c).wait_send()
        tcopy(CX, i, to_c, place[X]).wait_send()
        tcopy(CY, i, to_c, place[Y]).wait_send()
        tcopy(CD, i, to_c, place[D]).wait_send()
        if via_y(i):
            tcopy(D, i, to_y, place[X]).wait_send()
        else:
            tcopy(D, i, to_x, place[Y]).wait_send()


def on_device(S, Fn, tokens, projection, log_decay):
    rows, kf = tokens.shape
    ks, width = projection.shape[1:]
    Z = S // 2
    half = width // 2
    heads = half // HEAD
    nb = rows // BLK
    parts = 2 + heads
    dec = log_decay.T.reshape(2, heads * nb, BLK)
    dec = jnp.pad(dec, ((0, 0), (0, 8 - heads * nb), (0, 0)))
    dma = pltpu.SemaphoreType.DMA
    any_spec = pl.BlockSpec(memory_space=pl.ANY)
    return pl.pallas_call(
        functools.partial(kernel, S, Fn),
        out_shape=jax.ShapeDtypeStruct((rows, width), BF16),
        in_specs=[any_spec] * 3,
        out_specs=any_spec,
        scratch_shapes=[
            pltpu.VMEM((2 * Fn, rows, kf), BF16),
            pltpu.VMEM((3, Z, 2, ks, half), BF16),
            pltpu.VMEM((2, 8, BLK), F32),
            pltpu.VMEM((2, BLK, 8), F32),
            pltpu.VMEM((heads, 2 * nb, BLK, BLK), F32),
            pltpu.VMEM((2 * rows, half), BF16),
            pltpu.VMEM((2 * rows, half), BF16),
            pltpu.VMEM((heads, 2 * rows, HEAD), F32),
            pltpu.VMEM((heads, 2 * nb, HEAD, HEAD), F32),
            pltpu.VMEM((heads, 2 * nb, HEAD, HEAD), F32),
            pltpu.VMEM((heads, HEAD, HEAD), F32),
            pltpu.VMEM((heads, HEAD, HEAD), F32),
            pltpu.VMEM((heads, 2 * nb, BLK, HEAD), BF16),
            dma((7, PIECES)),
            dma((7, PIECES)),
            dma((parts,)),
            dma((parts,)),
            dma((parts,)),
            dma((parts, Z)),
            dma((parts, Z)),
            dma((parts, Z)),
            dma((6,)),
            dma((heads, nb)),
            dma((heads, nb)),
            dma((heads, nb)),
        ],
        compiler_params=pltpu.CompilerParams(
            collective_id=0, has_side_effects=True, vmem_limit_bytes=52 * 1024 * 1024
        ),
    )(tokens, projection, dec)


def solution(mesh):
    S, Fn = mesh.shape["seq"], mesh.shape["fsdp"]
    return jax.shard_map(
        functools.partial(on_device, S, Fn),
        mesh=mesh,
        in_specs=(P("seq", "fsdp"), P(None, "seq", "fsdp"), P("seq", "fsdp")),
        out_specs=P("seq", "fsdp"),
        check_vma=False,
    )
```

```python
import functools

import jax
import jax.numpy as jnp
from jax import lax
from jax.experimental import pallas as pl
from jax.experimental.pallas import tpu as pltpu
from jax.sharding import PartitionSpec as P

BLK = 512
HEAD = 128
PIECES = 4
MESH = pl.DeviceIdType.MESH
X, Y, D, C, CX, CY, CD = range(7)
F32 = jnp.float32
BF16 = jnp.bfloat16


def silu(v):
    return v / (1.0 + jnp.exp(-v))


def dot(a, b, dims=((1,), (0,))):
    return lax.dot_general(a, b, (dims, ((), ())), preferred_element_type=F32)


def split(v):
    high = v.astype(BF16)
    return high, (v - high.astype(F32)).astype(BF16)


def kernel(
    S,
    Fn,
    tok_in,
    proj_in,
    dec_in,
    out,
    tok,
    wts,
    dec,
    cols,
    fade,
    keys,
    vals,
    qacc,
    fresh,
    before,
    kvacc,
    enter,
    s_in,
    s_out,
    done,
    tsend,
    trecv,
    wloc,
    wysend,
    wyrecv,
    wrsend,
    wlsend,
    wrecv,
    misc,
    ssend,
    srecv,
    osend,
    orecv,
    oloc,
):
    Z = S // 2
    s, f = lax.axis_index("seq"), lax.axis_index("fsdp")
    z, y = s // 2, s % 2
    x, c = f // 2, f % 2
    rows, kf = tok_in.shape
    ks = proj_in.shape[1]
    half = proj_in.shape[2] // 2
    heads = half // HEAD
    nb = rows // BLK
    depth = 2 * ks
    prow = rows // PIECES

    to_x = (s, (1 - x) * 2 + c)
    to_y = (z * 2 + 1 - y, f)
    to_c = (s, x * 2 + 1 - c)
    to_r = (jnp.minimum(z + 1, Z - 1) * 2 + y, f)
    to_l = (jnp.maximum(z - 1, 0) * 2 + y, f)
    has_l, has_r = z > 0, z < Z - 1

    def shard(yy, xx, cc):
        return yy * Fn + xx * 2 + cc

    place = {
        X: shard(y, 1 - x, c),
        Y: shard(1 - y, x, c),
        D: shard(1 - y, 1 - x, c),
        C: shard(y, x, 1 - c),
        CX: shard(y, 1 - x, 1 - c),
        CY: shard(1 - y, x, 1 - c),
        CD: shard(1 - y, 1 - x, 1 - c),
    }
    mine = shard(y, x, c)

    def remote(src, dst, ssem, rsem, to):
        return pltpu.make_async_remote_copy(
            src_ref=src, dst_ref=dst, send_sem=ssem, recv_sem=rsem, device_id=to, device_id_type=MESH
        )

    barrier = pltpu.get_barrier_semaphore()
    for to in (to_x, to_y, to_c):
        pl.semaphore_signal(barrier, inc=1, device_id=to, device_id_type=MESH)

    for at in range(Z):

        @pl.when(at != z)
        def _(at=at):
            pl.semaphore_signal(barrier, inc=1, device_id=(at * 2 + y, f), device_id_type=MESH)

    pl.semaphore_wait(barrier, 3 + Z - 1)

    def tcopy(kind, i, to, at, src=None):
        here = tok.at[at, pl.ds(i * prow, prow)]
        return remote(here if src is None else src, here, tsend.at[kind, i], trecv.at[kind, i], to)

    def own_tok(kind, i, to):
        return tcopy(kind, i, to, mine, tok_in.at[pl.ds(i * prow, prow)])

    def got_tok(kind, i):
        tcopy(kind, i, to_c, place[kind]).wait_recv()

    def via_y(i):
        return i == PIECES - 1

    def side_step(i):
        got_tok(X, i)
        tcopy(CX, i, to_c, place[X]).start()
        if via_y(i):
            tcopy(D, i, to_y, place[X]).start()

    def pair_step(i):
        got_tok(Y, i)
        tcopy(CY, i, to_c, place[Y]).start()
        if not via_y(i):
            tcopy(D, i, to_x, place[Y]).start()

    def diag_step(i):
        got_tok(D, i)
        tcopy(CD, i, to_c, place[D]).start()

    parts = [(1, 0, half), (2, 0, half)]
    for h in range(heads):
        parts.append((0, h * HEAD, HEAD))

    def wslot(n, at):
        p, lo, width = parts[n]
        return wts.at[p, at, :, :, pl.ds(lo, width)]

    def wmember(n, yy):
        p, lo, width = parts[n]
        return wts.at[p, z, yy, :, pl.ds(lo, width)]

    def wsource(n, yy):
        p, lo, width = parts[n]
        return proj_in.at[p, :, pl.ds(pl.multiple_of(yy * half + lo, HEAD), width)]

    def wlocal(n):
        return pltpu.make_async_copy(wsource(n, y), wmember(n, y), wloc.at[n])

    def wpair(n):
        return remote(wsource(n, 1 - y), wmember(n, y), wysend.at[n], wyrecv.at[n], to_y)

    def wright(n, at):
        slot = wslot(n, at)
        return remote(slot, slot, wrsend.at[n, at], wrecv.at[n, at], to_r)

    def wleft(n, at):
        slot = wslot(n, at)
        return remote(slot, slot, wlsend.at[n, at], wrecv.at[n, at], to_l)

    def own_part(n):
        wlocal(n).wait()
        remote(wsource(n, y), wmember(n, 1 - y), wysend.at[n], wyrecv.at[n], to_y).wait_recv()

        @pl.when(has_r)
        def _():
            wright(n, z).start()

        @pl.when(has_l)
        def _():
            wleft(n, z).start()

    def wstep(n, d):
        @pl.when(z - d >= 0)
        def _():
            wright(n, z - d).wait_recv()

            @pl.when(has_r)
            def _():
                wright(n, z - d).start()

        @pl.when(z + d <= Z - 1)
        def _():
            wleft(n, z + d).wait_recv()

            @pl.when(has_l)
            def _():
                wleft(n, z + d).start()

    def wdirect(n, to):
        slot = wslot(n, z)
        return remote(slot, slot, wrsend.at[n, to], wrecv.at[n, z], (to * 2 + y, f))

    def own_query(n):
        wlocal(n).wait()
        remote(wsource(n, y), wmember(n, 1 - y), wysend.at[n], wyrecv.at[n], to_y).wait_recv()
        for to in range(Z):

            @pl.when(to != z)
            def _(to=to):
                wdirect(n, to).start()

    near = (z // (Z - 1)) * (Z - 1)
    far = Z - 1 - near

    def got_query(n, at):
        @pl.when(at != z)
        def _():
            wright(n, at).wait_recv()

    def got_near(n):
        got_query(n, near)
        for at in range(1, Z - 1):
            got_query(n, at)

    def wsteps(n, i):
        ends = (1, Z // 2, Z - 1, Z)
        for d in range(ends[i], ends[i + 1]):
            wstep(n, d)

    dec_copy = remote(dec_in.at[1 - y], dec.at[y], misc.at[0], misc.at[1], to_y)
    dec_copy.start()
    dec_local = pltpu.make_async_copy(dec_in.at[y], dec.at[y], misc.at[2])
    for n in (0, 1):
        wpair(n).start()
    for n in range(2):
        wlocal(n).start()
    for i in range(PIECES):
        own_tok(X, i, to_x).start()
        own_tok(Y, i, to_y).start()
    for i in range(PIECES):
        own_tok(C, i, to_c).start()
    for n in range(2, len(parts)):
        wlocal(n).start()
    tok_local = pltpu.make_async_copy(tok_in, tok.at[mine], misc.at[3])
    tok_local.start()
    own_part(0)
    own_part(1)

    dec_local.start()
    dec_local.wait()
    remote(dec_in.at[y], dec.at[1 - y], misc.at[0], misc.at[1], to_y).wait_recv()
    lane = lax.broadcasted_iota(jnp.int32, (8, BLK), 1)
    for yy in range(2):
        run = dec[yy]
        step = 1
        while step < BLK:
            run = run + jnp.where(lane >= step, pltpu.roll(run, step, 1), 0.0)
            step *= 2
        dec[yy] = run
        cols[yy] = run.T
    for h in range(heads):
        for b in range(nb):
            at = h * nb + b

            def fading(yy, _, h=h, b=b, at=at):
                gap = cols[yy, :, at : at + 1] - dec[yy, at : at + 1, :]
                t = lax.broadcasted_iota(jnp.int32, (BLK, BLK), 0)
                u = lax.broadcasted_iota(jnp.int32, (BLK, BLK), 1)
                fade[h, yy * nb + b] = jnp.exp(jnp.where(t >= u, gap, -1e30))
                return 0

            lax.fori_loop(0, 2, fading, 0)

    def chunk(n, yy, r, at):
        p, lo, width = parts[n]
        w = wts[p, at, :, :, lo : lo + width].reshape(depth, width)
        ff, off = (at * depth) // kf, (at * depth) % kf
        if depth == kf:
            return dot(tok[yy * Fn + ff, r, :], w)
        if not isinstance(at, int):
            off = pl.multiple_of(off, HEAD)
        return dot(tok[yy * Fn + ff, r, pl.ds(off, depth)], w)

    def partial(n, yy, r):
        total = chunk(n, yy, r, near)
        for at in range(1, Z - 1):
            total = total + chunk(n, yy, r, at)
        return total

    def begin(n, i):
        r = slice(i * BLK, (i + 1) * BLK)
        kvacc[n, r, :] = partial(n, y, pl.ds(i * BLK, BLK))

    def finish(n, yy, i, total):
        total = total + chunk(n, yy, pl.ds(i * BLK, BLK), far)
        to = pl.ds(pl.multiple_of(yy * rows + i * BLK, BLK), BLK)
        if n == 0:
            keys[to, :] = silu(total).astype(BF16)
        else:
            vals[to, :] = total.astype(BF16)

    def project(n, yy, i):
        finish(n, yy, i, partial(n, yy, pl.ds(i * BLK, BLK)))

    def states(yy, b):
        j = yy * nb + b
        r = pl.ds(pl.multiple_of(j * BLK, BLK), BLK)
        for h in range(heads):
            hc = slice(h * HEAD, (h + 1) * HEAD)
            at = h * nb + b
            run = cols[yy, :, at : at + 1]
            end = dec[yy, at : at + 1, BLK - 1 : BLK]
            high, low = split(keys[r, hc].astype(F32) * jnp.exp(end - run))
            v = vals[r, hc]
            fresh[h, j] = dot(high, v, ((0,), (0,))) + dot(low, v, ((0,), (0,)))

    def got_core(kinds, i):
        lo, hi = i * PIECES // nb, (i + 1) * PIECES // nb
        for j in range(lo, hi):
            for kind in kinds:
                got_tok(kind, j)

    def begin_query(h):
        def tile(i, _):
            yy, b = i // nb, i % nb
            r = pl.ds(pl.multiple_of(b * BLK, BLK), BLK)
            qacc[h, pl.ds(pl.multiple_of(i * BLK, BLK), BLK), :] = partial(2 + h, yy, r)
            return 0

        lax.fori_loop(0, 2 * nb, tile, 0)

    side_step(0)
    pair_step(0)
    wsteps(0, 0)
    wsteps(1, 0)
    for n in range(2, len(parts)):
        wpair(n).start()
    for i in range(1, PIECES - 1):
        side_step(i)
        pair_step(i)
    side_step(PIECES - 1)
    wsteps(0, 1)
    wsteps(1, 1)
    pair_step(PIECES - 1)
    for n in range(2, len(parts)):
        own_query(n)
    tok_local.wait()
    for i in range(nb):
        got_core((C, CX), i)
        begin(0, i)
        begin(1, i)
        if i == 0:
            diag_step(0)
    for i in range(1, PIECES // nb):
        diag_step(i)
    diag_step(PIECES - 1)
    wsteps(0, 2)
    wsteps(1, 2)
    for i in range(nb):
        finish(0, y, i, kvacc[0, i * BLK : (i + 1) * BLK, :])
        finish(1, y, i, kvacc[1, i * BLK : (i + 1) * BLK, :])
    got_core((CY, CD), 0)
    project(0, 1 - y, 0)
    project(1, 1 - y, 0)
    for i in range(PIECES // nb, PIECES - 1):
        diag_step(i)
    for b in range(nb):
        states(y, b)
    states(1 - y, 0)
    for i in range(1, nb):
        got_core((CY, CD), i)
        project(0, 1 - y, i)
        project(1, 1 - y, i)
        states(1 - y, i)

    def state_copy(to):
        return remote(
            s_out, s_in.at[z], ssend.at[to], srecv.at[z], (to * 2 + y, f)
        )

    def block_end(h, j):
        at = h * nb + j % nb
        return dec[j // nb, at : at + 1, BLK - 1 : BLK]

    for h in range(heads):
        state = jnp.zeros((HEAD, HEAD), F32)
        lead = jnp.zeros((1, 1), F32)
        for j in range(2 * nb):
            before[h, j] = state
            state = jnp.exp(block_end(h, j)) * state + fresh[h, j]
            lead = lead + block_end(h, j)
        s_out[h, 0:HEAD, :] = state
        s_out[h, HEAD : HEAD + 8, :] = jnp.broadcast_to(lead, (8, HEAD))
    for to in range(1, Z):

        @pl.when(to > z)
        def _(to=to):
            state_copy(to).start()

    for h in range(heads):
        got_near(2 + h)
        begin_query(h)

    enter[...] = jnp.zeros_like(enter)
    for at in range(Z - 1):

        @pl.when(at < z)
        def _(at=at):
            remote(s_out, s_in.at[at], ssend.at[at], srecv.at[at], (at * 2 + y, f)).wait_recv()
            for h in range(heads):
                decay = jnp.exp(s_in[at, h, HEAD : HEAD + 1, :])
                enter[h] = decay * enter[h] + s_in[at, h, 0:HEAD, :]

    for h in range(heads):
        lead = jnp.zeros((1, 1), F32)
        for j in range(2 * nb):
            before[h, j] = before[h, j] + jnp.exp(lead) * enter[h]
            lead = lead + block_end(h, j)

    def place_out(h, b, who):
        return out.at[
            pl.ds(b * BLK, BLK), pl.ds(pl.multiple_of(who * half + h * HEAD, HEAD), HEAD)
        ]

    def give(h, b):
        src = done.at[h, (1 - y) * nb + b]
        return remote(src, place_out(h, b, y), osend.at[h, b], orecv.at[h, b], to_y)

    def keep(h, b):
        return pltpu.make_async_copy(done.at[h, y * nb + b], place_out(h, b, y), oloc.at[h, b])

    def attend(h, yy, b):
        at = h * nb + b
        j = yy * nb + b
        hc = slice(h * HEAD, (h + 1) * HEAD)
        r = pl.ds(pl.multiple_of(j * BLK, BLK), BLK)
        total = qacc[h, r, :] + chunk(2 + h, yy, pl.ds(b * BLK, BLK), far)
        q, k, v = silu(total).astype(BF16), keys[r, hc], vals[r, hc]
        scores = dot(q, k, ((1,), (1,)))
        weights = (fade[h, j] * scores).astype(BF16)
        high, low = split(before[h, j])
        inter = dot(q, jnp.concatenate([high, low], axis=1))
        inter = inter[:, :HEAD] + inter[:, HEAD:]
        mixed = dot(weights, v) + jnp.exp(cols[yy, :, at : at + 1]) * inter
        scale = lax.rsqrt(jnp.mean(mixed * mixed, axis=-1, keepdims=True) + 1e-6)
        done[h, j] = (mixed * scale).astype(BF16)

    for h in range(heads):
        got_query(2 + h, far)
        for b in range(nb):
            attend(h, 1 - y, b)
            give(h, b).start()
    for h in range(heads):
        for b in range(nb):
            attend(h, y, b)
            keep(h, b).start()

    for h in range(heads):
        for b in range(nb):
            keep(h, b).wait()
            give(h, b).wait_send()
            remote(
                done.at[h, y * nb + b],
                place_out(h, b, 1 - y),
                osend.at[h, b],
                orecv.at[h, b],
                to_y,
            ).wait_recv()

    for to in range(1, Z):

        @pl.when(to > z)
        def _(to=to):
            state_copy(to).wait_send()

    dec_copy.wait_send()
    for n in range(len(parts)):
        wpair(n).wait_send()
    for n in range(2):
        for at in range(Z):

            @pl.when(has_r & (at <= z))
            def _(at=at):
                wright(n, at).wait_send()

            @pl.when(has_l & (at >= z))
            def _(at=at):
                wleft(n, at).wait_send()

    for n in range(2, len(parts)):
        for to in range(Z):

            @pl.when(to != z)
            def _(to=to):
                wdirect(n, to).wait_send()

    for i in range(PIECES):
        own_tok(X, i, to_x).wait_send()
        own_tok(Y, i, to_y).wait_send()
        own_tok(C, i, to_c).wait_send()
        tcopy(CX, i, to_c, place[X]).wait_send()
        tcopy(CY, i, to_c, place[Y]).wait_send()
        tcopy(CD, i, to_c, place[D]).wait_send()
        if via_y(i):
            tcopy(D, i, to_y, place[X]).wait_send()
        else:
            tcopy(D, i, to_x, place[Y]).wait_send()


def on_device(S, Fn, tokens, projection, log_decay):
    rows, kf = tokens.shape
    ks, width = projection.shape[1:]
    Z = S // 2
    half = width // 2
    heads = half // HEAD
    nb = rows // BLK
    parts = 2 + heads
    dec = log_decay.T.reshape(2, heads * nb, BLK)
    dec = jnp.pad(dec, ((0, 0), (0, 8 - heads * nb), (0, 0)))
    dma = pltpu.SemaphoreType.DMA
    any_spec = pl.BlockSpec(memory_space=pl.ANY)
    return pl.pallas_call(
        functools.partial(kernel, S, Fn),
        out_shape=jax.ShapeDtypeStruct((rows, width), BF16),
        in_specs=[any_spec] * 3,
        out_specs=any_spec,
        scratch_shapes=[
            pltpu.VMEM((2 * Fn, rows, kf), BF16),
            pltpu.VMEM((3, Z, 2, ks, half), BF16),
            pltpu.VMEM((2, 8, BLK), F32),
            pltpu.VMEM((2, BLK, 8), F32),
            pltpu.VMEM((heads, 2 * nb, BLK, BLK), F32),
            pltpu.VMEM((2 * rows, half), BF16),
            pltpu.VMEM((2 * rows, half), BF16),
            pltpu.VMEM((heads, 2 * rows, HEAD), F32),
            pltpu.VMEM((heads, 2 * nb, HEAD, HEAD), F32),
            pltpu.VMEM((heads, 2 * nb, HEAD, HEAD), F32),
            pltpu.VMEM((2, rows, half), F32),
            pltpu.VMEM((heads, HEAD, HEAD), F32),
            pltpu.VMEM((Z, heads, HEAD + 8, HEAD), F32),
            pltpu.VMEM((heads, HEAD + 8, HEAD), F32),
            pltpu.VMEM((heads, 2 * nb, BLK, HEAD), BF16),
            dma((7, PIECES)),
            dma((7, PIECES)),
            dma((parts,)),
            dma((parts,)),
            dma((parts,)),
            dma((parts, Z)),
            dma((parts, Z)),
            dma((parts, Z)),
            dma((4,)),
            dma((Z,)),
            dma((Z,)),
            dma((heads, nb)),
            dma((heads, nb)),
            dma((heads, nb)),
        ],
        compiler_params=pltpu.CompilerParams(
            collective_id=0, has_side_effects=True, vmem_limit_bytes=52 * 1024 * 1024
        ),
    )(tokens, projection, dec)


def solution(mesh):
    S, Fn = mesh.shape["seq"], mesh.shape["fsdp"]
    return jax.shard_map(
        functools.partial(on_device, S, Fn),
        mesh=mesh,
        in_specs=(P("seq", "fsdp"), P(None, "seq", "fsdp"), P("seq", "fsdp")),
        out_specs=P("seq", "fsdp"),
        check_vma=False,
    )
```

```python
import functools

import jax
import jax.numpy as jnp
from jax import lax
from jax.experimental import pallas as pl
from jax.experimental.pallas import tpu as pltpu
from jax.sharding import PartitionSpec as P

BLK = 512
HEAD = 128
PIECES = 4
MESH = pl.DeviceIdType.MESH
X, Y, D, C, CX, CY, CD = range(7)
F32 = jnp.float32
BF16 = jnp.bfloat16


def silu(v):
    return v / (1.0 + jnp.exp(-v))


def dot(a, b, dims=((1,), (0,))):
    return lax.dot_general(a, b, (dims, ((), ())), preferred_element_type=F32)


def split(v):
    high = v.astype(BF16)
    return high, (v - high.astype(F32)).astype(BF16)


def kernel(
    S,
    Fn,
    tok_in,
    proj_in,
    dec_in,
    out,
    tok,
    wts,
    dec,
    cols,
    fade,
    keys,
    vals,
    qacc,
    fresh,
    before,
    kvacc,
    enter,
    s_in,
    s_out,
    done,
    tsend,
    trecv,
    wloc,
    wysend,
    wyrecv,
    wrsend,
    wlsend,
    wrecv,
    misc,
    ssend,
    srecv,
    osend,
    orecv,
    oloc,
):
    Z = S // 2
    s, f = lax.axis_index("seq"), lax.axis_index("fsdp")
    z, y = s // 2, s % 2
    x, c = f // 2, f % 2
    rows, kf = tok_in.shape
    ks = proj_in.shape[1]
    half = proj_in.shape[2] // 2
    heads = half // HEAD
    nb = rows // BLK
    depth = 2 * ks
    prow = rows // PIECES

    to_x = (s, (1 - x) * 2 + c)
    to_y = (z * 2 + 1 - y, f)
    to_c = (s, x * 2 + 1 - c)
    to_r = (jnp.minimum(z + 1, Z - 1) * 2 + y, f)
    to_l = (jnp.maximum(z - 1, 0) * 2 + y, f)
    has_l, has_r = z > 0, z < Z - 1

    def shard(yy, xx, cc):
        return yy * Fn + xx * 2 + cc

    place = {
        X: shard(y, 1 - x, c),
        Y: shard(1 - y, x, c),
        D: shard(1 - y, 1 - x, c),
        C: shard(y, x, 1 - c),
        CX: shard(y, 1 - x, 1 - c),
        CY: shard(1 - y, x, 1 - c),
        CD: shard(1 - y, 1 - x, 1 - c),
    }
    mine = shard(y, x, c)

    def remote(src, dst, ssem, rsem, to):
        return pltpu.make_async_remote_copy(
            src_ref=src, dst_ref=dst, send_sem=ssem, recv_sem=rsem, device_id=to, device_id_type=MESH
        )

    barrier = pltpu.get_barrier_semaphore()
    for to in (to_x, to_y, to_c):
        pl.semaphore_signal(barrier, inc=1, device_id=to, device_id_type=MESH)

    for at in range(Z):

        @pl.when(at != z)
        def _(at=at):
            pl.semaphore_signal(barrier, inc=1, device_id=(at * 2 + y, f), device_id_type=MESH)

    pl.semaphore_wait(barrier, 3 + Z - 1)

    def tcopy(kind, i, to, at, src=None):
        here = tok.at[at, pl.ds(i * prow, prow)]
        return remote(here if src is None else src, here, tsend.at[kind, i], trecv.at[kind, i], to)

    def own_tok(kind, i, to):
        return tcopy(kind, i, to, mine, tok_in.at[pl.ds(i * prow, prow)])

    def got_tok(kind, i):
        tcopy(kind, i, to_c, place[kind]).wait_recv()

    def via_y(i):
        return i == PIECES - 1

    def side_step(i):
        got_tok(X, i)
        tcopy(CX, i, to_c, place[X]).start()
        if via_y(i):
            tcopy(D, i, to_y, place[X]).start()

    def pair_step(i):
        got_tok(Y, i)
        tcopy(CY, i, to_c, place[Y]).start()
        if not via_y(i):
            tcopy(D, i, to_x, place[Y]).start()

    def diag_step(i):
        got_tok(D, i)
        tcopy(CD, i, to_c, place[D]).start()

    parts = [(1, 0, half), (2, 0, half), (0, 0, half)]

    def wslot(n, at):
        p, lo, width = parts[n]
        return wts.at[p, at, :, :, pl.ds(lo, width)]

    def wmember(n, yy):
        p, lo, width = parts[n]
        return wts.at[p, z, yy, :, pl.ds(lo, width)]

    def wsource(n, yy):
        p, lo, width = parts[n]
        return proj_in.at[p, :, pl.ds(pl.multiple_of(yy * half + lo, HEAD), width)]

    def wlocal(n):
        return pltpu.make_async_copy(wsource(n, y), wmember(n, y), wloc.at[n])

    def wpair(n):
        return remote(wsource(n, 1 - y), wmember(n, y), wysend.at[n], wyrecv.at[n], to_y)

    def wright(n, at):
        slot = wslot(n, at)
        return remote(slot, slot, wrsend.at[n, at], wrecv.at[n, at], to_r)

    def wleft(n, at):
        slot = wslot(n, at)
        return remote(slot, slot, wlsend.at[n, at], wrecv.at[n, at], to_l)

    def own_part(n):
        wlocal(n).wait()
        remote(wsource(n, y), wmember(n, 1 - y), wysend.at[n], wyrecv.at[n], to_y).wait_recv()

        @pl.when(has_r)
        def _():
            wright(n, z).start()

        @pl.when(has_l)
        def _():
            wleft(n, z).start()

    def wstep(n, d):
        @pl.when(z - d >= 0)
        def _():
            wright(n, z - d).wait_recv()

            @pl.when(has_r)
            def _():
                wright(n, z - d).start()

        @pl.when(z + d <= Z - 1)
        def _():
            wleft(n, z + d).wait_recv()

            @pl.when(has_l)
            def _():
                wleft(n, z + d).start()

    def wdirect(n, to):
        slot = wslot(n, z)
        return remote(slot, slot, wrsend.at[n, to], wrecv.at[n, z], (to * 2 + y, f))

    def own_query(n):
        wlocal(n).wait()
        remote(wsource(n, y), wmember(n, 1 - y), wysend.at[n], wyrecv.at[n], to_y).wait_recv()
        for to in range(Z):

            @pl.when(to != z)
            def _(to=to):
                wdirect(n, to).start()

    near = (z // (Z - 1)) * (Z - 1)
    far = Z - 1 - near

    def got_query(n, at):
        @pl.when(at != z)
        def _():
            wright(n, at).wait_recv()

    def got_near(n):
        got_query(n, near)
        for at in range(1, Z - 1):
            got_query(n, at)

    def wsteps(n, i):
        ends = (1, Z // 2, Z - 1, Z)
        for d in range(ends[i], ends[i + 1]):
            wstep(n, d)

    dec_copy = remote(dec_in.at[1 - y], dec.at[y], misc.at[0], misc.at[1], to_y)
    dec_copy.start()
    dec_local = pltpu.make_async_copy(dec_in.at[y], dec.at[y], misc.at[2])
    for n in (0, 1):
        wpair(n).start()
    for n in range(2):
        wlocal(n).start()
    for i in range(PIECES):
        own_tok(X, i, to_x).start()
        if not via_y(i):
            own_tok(Y, i, to_y).start()
    for i in range(PIECES):
        own_tok(C, i, to_c).start()
    for n in range(2, len(parts)):
        wlocal(n).start()
    tok_local = pltpu.make_async_copy(tok_in, tok.at[mine], misc.at[3])
    tok_local.start()
    own_part(0)
    own_part(1)

    dec_local.start()
    dec_local.wait()
    remote(dec_in.at[y], dec.at[1 - y], misc.at[0], misc.at[1], to_y).wait_recv()
    lane = lax.broadcasted_iota(jnp.int32, (8, BLK), 1)
    for yy in range(2):
        run = dec[yy]
        step = 1
        while step < BLK:
            run = run + jnp.where(lane >= step, pltpu.roll(run, step, 1), 0.0)
            step *= 2
        dec[yy] = run
        cols[yy] = run.T
    for h in range(heads):
        for b in range(nb):
            at = h * nb + b

            def fading(yy, _, h=h, b=b, at=at):
                gap = cols[yy, :, at : at + 1] - dec[yy, at : at + 1, :]
                t = lax.broadcasted_iota(jnp.int32, (BLK, BLK), 0)
                u = lax.broadcasted_iota(jnp.int32, (BLK, BLK), 1)
                fade[h, yy * nb + b] = jnp.exp(jnp.where(t >= u, gap, -1e30))
                return 0

            lax.fori_loop(0, 2, fading, 0)

    def chunk(n, yy, r, at):
        p, lo, width = parts[n]
        w = wts[p, at, :, :, lo : lo + width].reshape(depth, width)
        ff, off = (at * depth) // kf, (at * depth) % kf
        if depth == kf:
            return dot(tok[yy * Fn + ff, r, :], w)
        if not isinstance(at, int):
            off = pl.multiple_of(off, HEAD)
        return dot(tok[yy * Fn + ff, r, pl.ds(off, depth)], w)

    def partial(n, yy, r):
        total = chunk(n, yy, r, near)
        for at in range(1, Z - 1):
            total = total + chunk(n, yy, r, at)
        return total

    def begin(n, i):
        r = slice(i * BLK, (i + 1) * BLK)
        kvacc[n, r, :] = partial(n, y, pl.ds(i * BLK, BLK))

    def finish(n, yy, i, total):
        total = total + chunk(n, yy, pl.ds(i * BLK, BLK), far)
        to = pl.ds(pl.multiple_of(yy * rows + i * BLK, BLK), BLK)
        if n == 0:
            keys[to, :] = silu(total).astype(BF16)
        else:
            vals[to, :] = total.astype(BF16)

    def project(n, yy, i):
        finish(n, yy, i, partial(n, yy, pl.ds(i * BLK, BLK)))

    def states(yy, b):
        j = yy * nb + b
        r = pl.ds(pl.multiple_of(j * BLK, BLK), BLK)
        for h in range(heads):
            hc = slice(h * HEAD, (h + 1) * HEAD)
            at = h * nb + b
            run = cols[yy, :, at : at + 1]
            end = dec[yy, at : at + 1, BLK - 1 : BLK]
            high, low = split(keys[r, hc].astype(F32) * jnp.exp(end - run))
            v = vals[r, hc]
            fresh[h, j] = dot(high, v, ((0,), (0,))) + dot(low, v, ((0,), (0,)))

    def got_core(kinds, i):
        lo, hi = i * PIECES // nb, (i + 1) * PIECES // nb
        for j in range(lo, hi):
            for kind in kinds:
                got_tok(kind, j)

    def begin_query():
        def tile(i, _):
            yy, b = i // nb, i % nb
            r = pl.ds(pl.multiple_of(b * BLK, BLK), BLK)
            qacc[pl.ds(pl.multiple_of(i * BLK, BLK), BLK), :] = partial(2, yy, r)
            return 0

        lax.fori_loop(0, 2 * nb, tile, 0)

    wsteps(0, 0)
    wsteps(1, 0)
    side_step(0)
    pair_step(0)
    own_tok(Y, PIECES - 1, to_y).start()
    wpair(2).start()
    for i in range(1, PIECES - 1):
        side_step(i)
        pair_step(i)
    side_step(PIECES - 1)
    wsteps(0, 1)
    wsteps(1, 1)
    pair_step(PIECES - 1)
    own_query(2)
    tok_local.wait()
    for i in range(nb):
        got_core((C, CX), i)
        begin(0, i)
        begin(1, i)
        if i == 0:
            diag_step(0)
    for i in range(1, PIECES // nb):
        diag_step(i)
    diag_step(PIECES - 1)
    wsteps(0, 2)
    wsteps(1, 2)
    for i in range(nb):
        finish(0, y, i, kvacc[0, i * BLK : (i + 1) * BLK, :])
        finish(1, y, i, kvacc[1, i * BLK : (i + 1) * BLK, :])
    got_core((CY, CD), 0)
    project(0, 1 - y, 0)
    project(1, 1 - y, 0)
    for i in range(PIECES // nb, PIECES - 1):
        diag_step(i)
    for b in range(nb):
        states(y, b)
    states(1 - y, 0)
    for i in range(1, nb):
        got_core((CY, CD), i)
        project(0, 1 - y, i)
        project(1, 1 - y, i)
        states(1 - y, i)

    def state_copy(to):
        return remote(
            s_out, s_in.at[z], ssend.at[to], srecv.at[z], (to * 2 + y, f)
        )

    def block_end(h, j):
        at = h * nb + j % nb
        return dec[j // nb, at : at + 1, BLK - 1 : BLK]

    for h in range(heads):
        state = jnp.zeros((HEAD, HEAD), F32)
        lead = jnp.zeros((1, 1), F32)
        for j in range(2 * nb):
            before[h, j] = state
            state = jnp.exp(block_end(h, j)) * state + fresh[h, j]
            lead = lead + block_end(h, j)
        s_out[h, 0:HEAD, :] = state
        s_out[h, HEAD : HEAD + 8, :] = jnp.broadcast_to(lead, (8, HEAD))
    for to in range(1, Z):

        @pl.when(to > z)
        def _(to=to):
            state_copy(to).start()

    got_near(2)
    begin_query()

    enter[...] = jnp.zeros_like(enter)
    for at in range(Z - 1):

        @pl.when(at < z)
        def _(at=at):
            remote(s_out, s_in.at[at], ssend.at[at], srecv.at[at], (at * 2 + y, f)).wait_recv()
            for h in range(heads):
                decay = jnp.exp(s_in[at, h, HEAD : HEAD + 1, :])
                enter[h] = decay * enter[h] + s_in[at, h, 0:HEAD, :]

    for h in range(heads):
        lead = jnp.zeros((1, 1), F32)
        for j in range(2 * nb):
            before[h, j] = before[h, j] + jnp.exp(lead) * enter[h]
            lead = lead + block_end(h, j)

    def place_out(b, who):
        return out.at[pl.ds(b * BLK, BLK), pl.ds(pl.multiple_of(who * half, HEAD), half)]

    def give(b):
        src = done.at[(1 - y) * nb + b]
        return remote(src, place_out(b, y), osend.at[b], orecv.at[b], to_y)

    def keep(b):
        return pltpu.make_async_copy(done.at[y * nb + b], place_out(b, y), oloc.at[b])

    def attend(yy, b):
        j = yy * nb + b
        r = pl.ds(pl.multiple_of(j * BLK, BLK), BLK)
        queries = silu(qacc[r, :] + chunk(2, yy, pl.ds(b * BLK, BLK), far)).astype(BF16)
        for h in range(heads):
            at = h * nb + b
            hc = slice(h * HEAD, (h + 1) * HEAD)
            q, k, v = queries[:, hc], keys[r, hc], vals[r, hc]
            scores = dot(q, k, ((1,), (1,)))
            weights = (fade[h, j] * scores).astype(BF16)
            high, low = split(before[h, j])
            inter = dot(q, jnp.concatenate([high, low], axis=1))
            inter = inter[:, :HEAD] + inter[:, HEAD:]
            mixed = dot(weights, v) + jnp.exp(cols[yy, :, at : at + 1]) * inter
            scale = lax.rsqrt(jnp.mean(mixed * mixed, axis=-1, keepdims=True) + 1e-6)
            done[j, :, hc] = (mixed * scale).astype(BF16)

    got_query(2, far)
    for b in range(nb):
        attend(1 - y, b)
        give(b).start()
    for b in range(nb):
        attend(y, b)
        keep(b).start()

    for b in range(nb):
        keep(b).wait()
        give(b).wait_send()
        remote(
            done.at[y * nb + b], place_out(b, 1 - y), osend.at[b], orecv.at[b], to_y
        ).wait_recv()

    for to in range(1, Z):

        @pl.when(to > z)
        def _(to=to):
            state_copy(to).wait_send()

    dec_copy.wait_send()
    for n in range(len(parts)):
        wpair(n).wait_send()
    for n in range(2):
        for at in range(Z):

            @pl.when(has_r & (at <= z))
            def _(at=at):
                wright(n, at).wait_send()

            @pl.when(has_l & (at >= z))
            def _(at=at):
                wleft(n, at).wait_send()

    for n in range(2, len(parts)):
        for to in range(Z):

            @pl.when(to != z)
            def _(to=to):
                wdirect(n, to).wait_send()

    for i in range(PIECES):
        own_tok(X, i, to_x).wait_send()
        own_tok(Y, i, to_y).wait_send()
        own_tok(C, i, to_c).wait_send()
        tcopy(CX, i, to_c, place[X]).wait_send()
        tcopy(CY, i, to_c, place[Y]).wait_send()
        tcopy(CD, i, to_c, place[D]).wait_send()
        if via_y(i):
            tcopy(D, i, to_y, place[X]).wait_send()
        else:
            tcopy(D, i, to_x, place[Y]).wait_send()


def on_device(S, Fn, tokens, projection, log_decay):
    rows, kf = tokens.shape
    ks, width = projection.shape[1:]
    Z = S // 2
    half = width // 2
    heads = half // HEAD
    nb = rows // BLK
    parts = 3
    dec = log_decay.T.reshape(2, heads * nb, BLK)
    dec = jnp.pad(dec, ((0, 0), (0, 8 - heads * nb), (0, 0)))
    dma = pltpu.SemaphoreType.DMA
    any_spec = pl.BlockSpec(memory_space=pl.ANY)
    return pl.pallas_call(
        functools.partial(kernel, S, Fn),
        out_shape=jax.ShapeDtypeStruct((rows, width), BF16),
        in_specs=[any_spec] * 3,
        out_specs=any_spec,
        scratch_shapes=[
            pltpu.VMEM((2 * Fn, rows, kf), BF16),
            pltpu.VMEM((3, Z, 2, ks, half), BF16),
            pltpu.VMEM((2, 8, BLK), F32),
            pltpu.VMEM((2, BLK, 8), F32),
            pltpu.VMEM((heads, 2 * nb, BLK, BLK), F32),
            pltpu.VMEM((2 * rows, half), BF16),
            pltpu.VMEM((2 * rows, half), BF16),
            pltpu.VMEM((2 * rows, half), F32),
            pltpu.VMEM((heads, 2 * nb, HEAD, HEAD), F32),
            pltpu.VMEM((heads, 2 * nb, HEAD, HEAD), F32),
            pltpu.VMEM((2, rows, half), F32),
            pltpu.VMEM((heads, HEAD, HEAD), F32),
            pltpu.VMEM((Z, heads, HEAD + 8, HEAD), F32),
            pltpu.VMEM((heads, HEAD + 8, HEAD), F32),
            pltpu.VMEM((2 * nb, BLK, half), BF16),
            dma((7, PIECES)),
            dma((7, PIECES)),
            dma((parts,)),
            dma((parts,)),
            dma((parts,)),
            dma((parts, Z)),
            dma((parts, Z)),
            dma((parts, Z)),
            dma((4,)),
            dma((Z,)),
            dma((Z,)),
            dma((nb,)),
            dma((nb,)),
            dma((nb,)),
        ],
        compiler_params=pltpu.CompilerParams(
            collective_id=0, has_side_effects=True, vmem_limit_bytes=52 * 1024 * 1024
        ),
    )(tokens, projection, dec)


def solution(mesh):
    S, Fn = mesh.shape["seq"], mesh.shape["fsdp"]
    return jax.shard_map(
        functools.partial(on_device, S, Fn),
        mesh=mesh,
        in_specs=(P("seq", "fsdp"), P(None, "seq", "fsdp"), P("seq", "fsdp")),
        out_specs=P("seq", "fsdp"),
        check_vma=False,
    )
```

```python
import functools

import jax
import jax.numpy as jnp
from jax import lax
from jax.experimental import pallas as pl
from jax.experimental.pallas import tpu as pltpu
from jax.sharding import PartitionSpec as P

BLK = 512
HEAD = 128
PIECES = 4
MESH = pl.DeviceIdType.MESH
X, Y, D, C, CX, CY, CD = range(7)
F32 = jnp.float32
BF16 = jnp.bfloat16


def silu(v):
    return v / (1.0 + jnp.exp(-v))


def dot(a, b, dims=((1,), (0,))):
    return lax.dot_general(a, b, (dims, ((), ())), preferred_element_type=F32)


def split(v):
    high = v.astype(BF16)
    return high, (v - high.astype(F32)).astype(BF16)


def kernel(
    S,
    Fn,
    tok_in,
    proj_in,
    dec_in,
    out,
    tok,
    wts,
    dec,
    cols,
    fade,
    keys,
    vals,
    qacc,
    fresh,
    before,
    kvacc,
    enter,
    s_in,
    s_out,
    done,
    tsend,
    trecv,
    wloc,
    wysend,
    wyrecv,
    wrsend,
    wlsend,
    wrecv,
    misc,
    ssend,
    srecv,
    osend,
    orecv,
    oloc,
):
    Z = S // 2
    s, f = lax.axis_index("seq"), lax.axis_index("fsdp")
    z, y = s // 2, s % 2
    x, c = f // 2, f % 2
    rows, kf = tok_in.shape
    ks = proj_in.shape[1]
    half = proj_in.shape[2] // 2
    heads = half // HEAD
    nb = rows // BLK
    depth = 2 * ks
    prow = rows // PIECES

    to_x = (s, (1 - x) * 2 + c)
    to_y = (z * 2 + 1 - y, f)
    to_c = (s, x * 2 + 1 - c)
    to_r = (jnp.minimum(z + 1, Z - 1) * 2 + y, f)
    to_l = (jnp.maximum(z - 1, 0) * 2 + y, f)
    has_l, has_r = z > 0, z < Z - 1

    def shard(yy, xx, cc):
        return yy * Fn + xx * 2 + cc

    place = {
        X: shard(y, 1 - x, c),
        Y: shard(1 - y, x, c),
        D: shard(1 - y, 1 - x, c),
        C: shard(y, x, 1 - c),
        CX: shard(y, 1 - x, 1 - c),
        CY: shard(1 - y, x, 1 - c),
        CD: shard(1 - y, 1 - x, 1 - c),
    }
    mine = shard(y, x, c)

    def remote(src, dst, ssem, rsem, to):
        return pltpu.make_async_remote_copy(
            src_ref=src, dst_ref=dst, send_sem=ssem, recv_sem=rsem, device_id=to, device_id_type=MESH
        )

    barrier = pltpu.get_barrier_semaphore()
    for to in (to_x, to_y, to_c):
        pl.semaphore_signal(barrier, inc=1, device_id=to, device_id_type=MESH)

    for at in range(Z):

        @pl.when(at != z)
        def _(at=at):
            pl.semaphore_signal(barrier, inc=1, device_id=(at * 2 + y, f), device_id_type=MESH)

    pl.semaphore_wait(barrier, 3 + Z - 1)

    def tcopy(kind, i, to, at, src=None):
        here = tok.at[at, pl.ds(i * prow, prow)]
        return remote(here if src is None else src, here, tsend.at[kind, i], trecv.at[kind, i], to)

    def own_tok(kind, i, to):
        return tcopy(kind, i, to, mine, tok_in.at[pl.ds(i * prow, prow)])

    def got_tok(kind, i):
        tcopy(kind, i, to_c, place[kind]).wait_recv()

    def via_y(i):
        return i == PIECES - 1

    def side_step(i):
        got_tok(X, i)
        tcopy(CX, i, to_c, place[X]).start()
        if via_y(i):
            tcopy(D, i, to_y, place[X]).start()

    def pair_step(i):
        got_tok(Y, i)
        tcopy(CY, i, to_c, place[Y]).start()
        if not via_y(i):
            tcopy(D, i, to_x, place[Y]).start()

    def diag_step(i):
        got_tok(D, i)
        tcopy(CD, i, to_c, place[D]).start()

    parts = [(1, 0, half), (2, 0, half), (0, 0, half)]

    def wslot(n, at, yy):
        p, lo, width = parts[n]
        return wts.at[p, at, yy, :, pl.ds(lo, width)]

    def wmember(n, yy):
        p, lo, width = parts[n]
        return wts.at[p, z, yy, :, pl.ds(lo, width)]

    def wsource(n, yy):
        p, lo, width = parts[n]
        return proj_in.at[p, :, pl.ds(pl.multiple_of(yy * half + lo, HEAD), width)]

    def wlocal(n):
        return pltpu.make_async_copy(wsource(n, y), wmember(n, y), wloc.at[n])

    def wpair(n):
        return remote(wsource(n, 1 - y), wmember(n, y), wysend.at[n], wyrecv.at[n], to_y)

    def wright(n, at, yy):
        slot = wslot(n, at, yy)
        return remote(slot, slot, wrsend.at[n, at, yy], wrecv.at[n, at, yy], to_r)

    def wleft(n, at, yy):
        slot = wslot(n, at, yy)
        return remote(slot, slot, wlsend.at[n, at, yy], wrecv.at[n, at, yy], to_l)

    def got_pair(n):
        remote(wsource(n, y), wmember(n, 1 - y), wysend.at[n], wyrecv.at[n], to_y).wait_recv()

    def own_part(n, yy):
        @pl.when(has_r)
        def _():
            wright(n, z, yy).start()

        @pl.when(has_l)
        def _():
            wleft(n, z, yy).start()

    def wstep(n, d):
        for yy in (y, 1 - y):

            @pl.when(z - d >= 0)
            def _(yy=yy):
                wright(n, z - d, yy).wait_recv()

                @pl.when(has_r)
                def _():
                    wright(n, z - d, yy).start()

            @pl.when(z + d <= Z - 1)
            def _(yy=yy):
                wleft(n, z + d, yy).wait_recv()

                @pl.when(has_l)
                def _():
                    wleft(n, z + d, yy).start()

    def wdirect(n, to, yy):
        slot = wslot(n, z, yy)
        return remote(slot, slot, wrsend.at[n, to, yy], wrecv.at[n, z, yy], (to * 2 + y, f))

    def own_query(n):
        wlocal(n).wait()
        got_pair(n)
        for to in range(Z):

            @pl.when(to != z)
            def _(to=to):
                for yy in range(2):
                    wdirect(n, to, yy).start()

    near = (z // (Z - 1)) * (Z - 1)
    far = Z - 1 - near

    def got_query(n, at):
        @pl.when(at != z)
        def _():
            for yy in range(2):
                wright(n, at, yy).wait_recv()

    def got_near(n):
        got_query(n, near)
        for at in range(1, Z - 1):
            got_query(n, at)

    def wsteps(n, i):
        ends = (1, Z // 2, Z - 1, Z)
        for d in range(ends[i], ends[i + 1]):
            wstep(n, d)

    dec_copy = remote(dec_in.at[1 - y], dec.at[y], misc.at[0], misc.at[1], to_y)
    dec_copy.start()
    dec_local = pltpu.make_async_copy(dec_in.at[y], dec.at[y], misc.at[2])
    for n in (0, 1):
        wpair(n).start()
        wlocal(n).start()
    for i in range(PIECES):
        own_tok(X, i, to_x).start()
    for n in (0, 1):
        wlocal(n).wait()
        own_part(n, y)
    for i in range(PIECES):
        own_tok(C, i, to_c).start()
    wlocal(2).start()
    tok_local = pltpu.make_async_copy(tok_in, tok.at[mine], misc.at[3])
    tok_local.start()
    for n in (0, 1):
        got_pair(n)
        own_part(n, 1 - y)
    for i in range(PIECES):
        if not via_y(i):
            own_tok(Y, i, to_y).start()

    dec_local.start()
    dec_local.wait()
    remote(dec_in.at[y], dec.at[1 - y], misc.at[0], misc.at[1], to_y).wait_recv()
    lane = lax.broadcasted_iota(jnp.int32, (8, BLK), 1)
    for yy in range(2):
        run = dec[yy]
        step = 1
        while step < BLK:
            run = run + jnp.where(lane >= step, pltpu.roll(run, step, 1), 0.0)
            step *= 2
        dec[yy] = run
        cols[yy] = run.T
    for h in range(heads):
        for b in range(nb):
            at = h * nb + b

            def fading(yy, _, h=h, b=b, at=at):
                gap = cols[yy, :, at : at + 1] - dec[yy, at : at + 1, :]
                t = lax.broadcasted_iota(jnp.int32, (BLK, BLK), 0)
                u = lax.broadcasted_iota(jnp.int32, (BLK, BLK), 1)
                fade[h, yy * nb + b] = jnp.exp(jnp.where(t >= u, gap, -1e30))
                return 0

            lax.fori_loop(0, 2, fading, 0)

    def chunk(n, yy, r, at):
        p, lo, width = parts[n]
        w = wts[p, at, :, :, lo : lo + width].reshape(depth, width)
        ff, off = (at * depth) // kf, (at * depth) % kf
        if depth == kf:
            return dot(tok[yy * Fn + ff, r, :], w)
        if not isinstance(at, int):
            off = pl.multiple_of(off, HEAD)
        return dot(tok[yy * Fn + ff, r, pl.ds(off, depth)], w)

    def partial(n, yy, r):
        total = chunk(n, yy, r, near)
        for at in range(1, Z - 1):
            total = total + chunk(n, yy, r, at)
        return total

    def begin(n, i):
        r = slice(i * BLK, (i + 1) * BLK)
        kvacc[n, r, :] = partial(n, y, pl.ds(i * BLK, BLK))

    def finish(n, yy, i, total):
        total = total + chunk(n, yy, pl.ds(i * BLK, BLK), far)
        to = pl.ds(pl.multiple_of(yy * rows + i * BLK, BLK), BLK)
        if n == 0:
            keys[to, :] = silu(total).astype(BF16)
        else:
            vals[to, :] = total.astype(BF16)

    def project(n, yy, i):
        finish(n, yy, i, partial(n, yy, pl.ds(i * BLK, BLK)))

    def states(yy, b):
        j = yy * nb + b
        r = pl.ds(pl.multiple_of(j * BLK, BLK), BLK)
        for h in range(heads):
            hc = slice(h * HEAD, (h + 1) * HEAD)
            at = h * nb + b
            run = cols[yy, :, at : at + 1]
            end = dec[yy, at : at + 1, BLK - 1 : BLK]
            high, low = split(keys[r, hc].astype(F32) * jnp.exp(end - run))
            v = vals[r, hc]
            fresh[h, j] = dot(high, v, ((0,), (0,))) + dot(low, v, ((0,), (0,)))

    def got_core(kinds, i):
        lo, hi = i * PIECES // nb, (i + 1) * PIECES // nb
        for j in range(lo, hi):
            for kind in kinds:
                got_tok(kind, j)

    def begin_query():
        def tile(i, _):
            yy, b = i // nb, i % nb
            r = pl.ds(pl.multiple_of(b * BLK, BLK), BLK)
            qacc[pl.ds(pl.multiple_of(i * BLK, BLK), BLK), :] = partial(2, yy, r)
            return 0

        lax.fori_loop(0, 2 * nb, tile, 0)

    wsteps(0, 0)
    wsteps(1, 0)
    side_step(0)
    pair_step(0)
    own_tok(Y, PIECES - 1, to_y).start()
    wpair(2).start()
    for i in range(1, PIECES - 1):
        side_step(i)
        pair_step(i)
    side_step(PIECES - 1)
    wsteps(0, 1)
    wsteps(1, 1)
    pair_step(PIECES - 1)
    own_query(2)
    tok_local.wait()
    for i in range(nb):
        got_core((C, CX), i)
        begin(0, i)
        begin(1, i)
        if i == 0:
            diag_step(0)
    for i in range(1, PIECES // nb):
        diag_step(i)
    diag_step(PIECES - 1)
    wsteps(0, 2)
    wsteps(1, 2)
    for i in range(nb):
        finish(0, y, i, kvacc[0, i * BLK : (i + 1) * BLK, :])
        finish(1, y, i, kvacc[1, i * BLK : (i + 1) * BLK, :])
    got_core((CY, CD), 0)
    project(0, 1 - y, 0)
    project(1, 1 - y, 0)
    for i in range(PIECES // nb, PIECES - 1):
        diag_step(i)
    for b in range(nb):
        states(y, b)
    states(1 - y, 0)
    for i in range(1, nb):
        got_core((CY, CD), i)
        project(0, 1 - y, i)
        project(1, 1 - y, i)
        states(1 - y, i)

    def state_copy(to):
        return remote(
            s_out, s_in.at[z], ssend.at[to], srecv.at[z], (to * 2 + y, f)
        )

    def block_end(h, j):
        at = h * nb + j % nb
        return dec[j // nb, at : at + 1, BLK - 1 : BLK]

    for h in range(heads):
        state = jnp.zeros((HEAD, HEAD), F32)
        lead = jnp.zeros((1, 1), F32)
        for j in range(2 * nb):
            before[h, j] = state
            state = jnp.exp(block_end(h, j)) * state + fresh[h, j]
            lead = lead + block_end(h, j)
        s_out[h, 0:HEAD, :] = state
        s_out[h, HEAD : HEAD + 8, :] = jnp.broadcast_to(lead, (8, HEAD))
    for to in range(1, Z):

        @pl.when(to > z)
        def _(to=to):
            state_copy(to).start()

    got_near(2)
    begin_query()

    enter[...] = jnp.zeros_like(enter)
    for at in range(Z - 1):

        @pl.when(at < z)
        def _(at=at):
            remote(s_out, s_in.at[at], ssend.at[at], srecv.at[at], (at * 2 + y, f)).wait_recv()
            for h in range(heads):
                decay = jnp.exp(s_in[at, h, HEAD : HEAD + 1, :])
                enter[h] = decay * enter[h] + s_in[at, h, 0:HEAD, :]

    for h in range(heads):
        lead = jnp.zeros((1, 1), F32)
        for j in range(2 * nb):
            before[h, j] = before[h, j] + jnp.exp(lead) * enter[h]
            lead = lead + block_end(h, j)

    def place_out(b, who):
        return out.at[pl.ds(b * BLK, BLK), pl.ds(pl.multiple_of(who * half, HEAD), half)]

    def give(b):
        src = done.at[(1 - y) * nb + b]
        return remote(src, place_out(b, y), osend.at[b], orecv.at[b], to_y)

    def keep(b):
        return pltpu.make_async_copy(done.at[y * nb + b], place_out(b, y), oloc.at[b])

    def attend(yy, b):
        j = yy * nb + b
        r = pl.ds(pl.multiple_of(j * BLK, BLK), BLK)
        queries = silu(qacc[r, :] + chunk(2, yy, pl.ds(b * BLK, BLK), far)).astype(BF16)
        for h in range(heads):
            at = h * nb + b
            hc = slice(h * HEAD, (h + 1) * HEAD)
            q, k, v = queries[:, hc], keys[r, hc], vals[r, hc]
            scores = dot(q, k, ((1,), (1,)))
            weights = (fade[h, j] * scores).astype(BF16)
            high, low = split(before[h, j])
            inter = dot(q, jnp.concatenate([high, low], axis=1))
            inter = inter[:, :HEAD] + inter[:, HEAD:]
            mixed = dot(weights, v) + jnp.exp(cols[yy, :, at : at + 1]) * inter
            scale = lax.rsqrt(jnp.mean(mixed * mixed, axis=-1, keepdims=True) + 1e-6)
            done[j, :, hc] = (mixed * scale).astype(BF16)

    got_query(2, far)
    for b in range(nb):
        attend(1 - y, b)
        give(b).start()
    for b in range(nb):
        attend(y, b)
        keep(b).start()

    for b in range(nb):
        keep(b).wait()
        give(b).wait_send()
        remote(
            done.at[y * nb + b], place_out(b, 1 - y), osend.at[b], orecv.at[b], to_y
        ).wait_recv()

    for to in range(1, Z):

        @pl.when(to > z)
        def _(to=to):
            state_copy(to).wait_send()

    dec_copy.wait_send()
    for n in range(len(parts)):
        wpair(n).wait_send()
    for at in range(Z):
        for n in range(2):
            for yy in range(2):

                @pl.when(has_r & (at <= z))
                def _(n=n, at=at, yy=yy):
                    wright(n, at, yy).wait_send()

                @pl.when(has_l & (at >= z))
                def _(n=n, at=at, yy=yy):
                    wleft(n, at, yy).wait_send()

        @pl.when(at != z)
        def _(at=at):
            for yy in range(2):
                wdirect(2, at, yy).wait_send()

    for i in range(PIECES):
        own_tok(X, i, to_x).wait_send()
        own_tok(Y, i, to_y).wait_send()
        own_tok(C, i, to_c).wait_send()
        tcopy(CX, i, to_c, place[X]).wait_send()
        tcopy(CY, i, to_c, place[Y]).wait_send()
        tcopy(CD, i, to_c, place[D]).wait_send()
        if via_y(i):
            tcopy(D, i, to_y, place[X]).wait_send()
        else:
            tcopy(D, i, to_x, place[Y]).wait_send()


def on_device(S, Fn, tokens, projection, log_decay):
    rows, kf = tokens.shape
    ks, width = projection.shape[1:]
    Z = S // 2
    half = width // 2
    heads = half // HEAD
    nb = rows // BLK
    parts = 3
    dec = log_decay.T.reshape(2, heads * nb, BLK)
    dec = jnp.pad(dec, ((0, 0), (0, 8 - heads * nb), (0, 0)))
    dma = pltpu.SemaphoreType.DMA
    any_spec = pl.BlockSpec(memory_space=pl.ANY)
    return pl.pallas_call(
        functools.partial(kernel, S, Fn),
        out_shape=jax.ShapeDtypeStruct((rows, width), BF16),
        in_specs=[any_spec] * 3,
        out_specs=any_spec,
        scratch_shapes=[
            pltpu.VMEM((2 * Fn, rows, kf), BF16),
            pltpu.VMEM((3, Z, 2, ks, half), BF16),
            pltpu.VMEM((2, 8, BLK), F32),
            pltpu.VMEM((2, BLK, 8), F32),
            pltpu.VMEM((heads, 2 * nb, BLK, BLK), F32),
            pltpu.VMEM((2 * rows, half), BF16),
            pltpu.VMEM((2 * rows, half), BF16),
            pltpu.VMEM((2 * rows, half), F32),
            pltpu.VMEM((heads, 2 * nb, HEAD, HEAD), F32),
            pltpu.VMEM((heads, 2 * nb, HEAD, HEAD), F32),
            pltpu.VMEM((2, rows, half), F32),
            pltpu.VMEM((heads, HEAD, HEAD), F32),
            pltpu.VMEM((Z, heads, HEAD + 8, HEAD), F32),
            pltpu.VMEM((heads, HEAD + 8, HEAD), F32),
            pltpu.VMEM((2 * nb, BLK, half), BF16),
            dma((7, PIECES)),
            dma((7, PIECES)),
            dma((parts,)),
            dma((parts,)),
            dma((parts,)),
            dma((parts, Z, 2)),
            dma((parts, Z, 2)),
            dma((parts, Z, 2)),
            dma((4,)),
            dma((Z,)),
            dma((Z,)),
            dma((nb,)),
            dma((nb,)),
            dma((nb,)),
        ],
        compiler_params=pltpu.CompilerParams(
            collective_id=0, has_side_effects=True, vmem_limit_bytes=52 * 1024 * 1024
        ),
    )(tokens, projection, dec)


def solution(mesh):
    S, Fn = mesh.shape["seq"], mesh.shape["fsdp"]
    return jax.shard_map(
        functools.partial(on_device, S, Fn),
        mesh=mesh,
        in_specs=(P("seq", "fsdp"), P(None, "seq", "fsdp"), P("seq", "fsdp")),
        out_specs=P("seq", "fsdp"),
        check_vma=False,
    )
```

```python
import functools

import jax
import jax.numpy as jnp
from jax import lax
from jax.experimental import pallas as pl
from jax.experimental.pallas import tpu as pltpu
from jax.sharding import PartitionSpec as P

BLK = 512
HEAD = 128
PIECES = 4
MESH = pl.DeviceIdType.MESH
X, Y, D, C, CX, CY, CD = range(7)
F32 = jnp.float32
BF16 = jnp.bfloat16


def silu(v):
    return v / (1.0 + jnp.exp(-v))


def dot(a, b, dims=((1,), (0,))):
    return lax.dot_general(a, b, (dims, ((), ())), preferred_element_type=F32)


def split(v):
    high = v.astype(BF16)
    return high, (v - high.astype(F32)).astype(BF16)


def kernel(
    S,
    Fn,
    tok_in,
    proj_in,
    dec_in,
    out,
    tok,
    wts,
    dec,
    cols,
    fade,
    keys,
    vals,
    qacc,
    qry,
    fresh,
    before,
    kvacc,
    enter,
    s_in,
    s_out,
    done,
    tsend,
    trecv,
    wloc,
    wysend,
    wyrecv,
    wrsend,
    wlsend,
    wrecv,
    misc,
    ssend,
    srecv,
    osend,
    orecv,
    oloc,
):
    Z = S // 2
    s, f = lax.axis_index("seq"), lax.axis_index("fsdp")
    z, y = s // 2, s % 2
    x, c = f // 2, f % 2
    rows, kf = tok_in.shape
    ks = proj_in.shape[1]
    half = proj_in.shape[2] // 2
    heads = half // HEAD
    nb = rows // BLK
    depth = 2 * ks
    prow = rows // PIECES

    to_x = (s, (1 - x) * 2 + c)
    to_y = (z * 2 + 1 - y, f)
    to_c = (s, x * 2 + 1 - c)
    to_r = (jnp.minimum(z + 1, Z - 1) * 2 + y, f)
    to_l = (jnp.maximum(z - 1, 0) * 2 + y, f)
    has_l, has_r = z > 0, z < Z - 1

    def shard(yy, xx, cc):
        return yy * Fn + xx * 2 + cc

    place = {
        X: shard(y, 1 - x, c),
        Y: shard(1 - y, x, c),
        D: shard(1 - y, 1 - x, c),
        C: shard(y, x, 1 - c),
        CX: shard(y, 1 - x, 1 - c),
        CY: shard(1 - y, x, 1 - c),
        CD: shard(1 - y, 1 - x, 1 - c),
    }
    mine = shard(y, x, c)

    def remote(src, dst, ssem, rsem, to):
        return pltpu.make_async_remote_copy(
            src_ref=src, dst_ref=dst, send_sem=ssem, recv_sem=rsem, device_id=to, device_id_type=MESH
        )

    barrier = pltpu.get_barrier_semaphore()
    for to in (to_x, to_y, to_c):
        pl.semaphore_signal(barrier, inc=1, device_id=to, device_id_type=MESH)

    for at in range(Z):

        @pl.when(at != z)
        def _(at=at):
            pl.semaphore_signal(barrier, inc=1, device_id=(at * 2 + y, f), device_id_type=MESH)

    pl.semaphore_wait(barrier, 3 + Z - 1)

    def tcopy(kind, i, to, at, src=None):
        here = tok.at[at, pl.ds(i * prow, prow)]
        return remote(here if src is None else src, here, tsend.at[kind, i], trecv.at[kind, i], to)

    def own_tok(kind, i, to):
        return tcopy(kind, i, to, mine, tok_in.at[pl.ds(i * prow, prow)])

    def got_tok(kind, i):
        tcopy(kind, i, to_c, place[kind]).wait_recv()

    def via_y(i):
        return i == PIECES - 1

    def side_step(i):
        got_tok(X, i)
        tcopy(CX, i, to_c, place[X]).start()
        if via_y(i):
            tcopy(D, i, to_y, place[X]).start()

    def pair_step(i):
        got_tok(Y, i)
        tcopy(CY, i, to_c, place[Y]).start()
        if not via_y(i):
            tcopy(D, i, to_x, place[Y]).start()

    def diag_step(i):
        got_tok(D, i)
        tcopy(CD, i, to_c, place[D]).start()

    parts = [(1, 0, half), (2, 0, half), (0, 0, half)]

    def wslot(n, at, yy):
        p, lo, width = parts[n]
        return wts.at[p, at, yy, :, pl.ds(lo, width)]

    def wmember(n, yy):
        p, lo, width = parts[n]
        return wts.at[p, z, yy, :, pl.ds(lo, width)]

    def wsource(n, yy):
        p, lo, width = parts[n]
        return proj_in.at[p, :, pl.ds(pl.multiple_of(yy * half + lo, HEAD), width)]

    def wlocal(n):
        return pltpu.make_async_copy(wsource(n, y), wmember(n, y), wloc.at[n])

    def wpair(n):
        return remote(wsource(n, 1 - y), wmember(n, y), wysend.at[n], wyrecv.at[n], to_y)

    def wright(n, at, yy):
        slot = wslot(n, at, yy)
        return remote(slot, slot, wrsend.at[n, at, yy], wrecv.at[n, at, yy], to_r)

    def wleft(n, at, yy):
        slot = wslot(n, at, yy)
        return remote(slot, slot, wlsend.at[n, at, yy], wrecv.at[n, at, yy], to_l)

    def got_pair(n):
        remote(wsource(n, y), wmember(n, 1 - y), wysend.at[n], wyrecv.at[n], to_y).wait_recv()

    def own_part(n, yy):
        @pl.when(has_r)
        def _():
            wright(n, z, yy).start()

        @pl.when(has_l)
        def _():
            wleft(n, z, yy).start()

    def wstep(n, d):
        for yy in (y, 1 - y):

            @pl.when(z - d >= 0)
            def _(yy=yy):
                wright(n, z - d, yy).wait_recv()

                @pl.when(has_r)
                def _():
                    wright(n, z - d, yy).start()

            @pl.when(z + d <= Z - 1)
            def _(yy=yy):
                wleft(n, z + d, yy).wait_recv()

                @pl.when(has_l)
                def _():
                    wleft(n, z + d, yy).start()

    def wdirect(n, to, yy):
        slot = wslot(n, z, yy)
        return remote(slot, slot, wrsend.at[n, to, yy], wrecv.at[n, z, yy], (to * 2 + y, f))

    def own_query(n):
        wlocal(n).wait()
        got_pair(n)
        for to in range(Z):

            @pl.when(to != z)
            def _(to=to):
                for yy in range(2):
                    wdirect(n, to, yy).start()

    near = (z // (Z - 1)) * (Z - 1)
    far = Z - 1 - near

    def got_query(n, at):
        @pl.when(at != z)
        def _():
            for yy in range(2):
                wright(n, at, yy).wait_recv()

    def got_near(n):
        got_query(n, near)
        for at in range(1, Z - 1):
            got_query(n, at)

    def wsteps(n, i):
        ends = (1, Z // 2, Z - 1, Z)
        for d in range(ends[i], ends[i + 1]):
            wstep(n, d)

    dec_copy = remote(dec_in.at[1 - y], dec.at[y], misc.at[0], misc.at[1], to_y)
    dec_copy.start()
    dec_local = pltpu.make_async_copy(dec_in.at[y], dec.at[y], misc.at[2])
    for n in (0, 1):
        wpair(n).start()
        wlocal(n).start()
    for i in range(PIECES):
        own_tok(X, i, to_x).start()
    for n in (0, 1):
        wlocal(n).wait()
        own_part(n, y)
    for i in range(PIECES):
        own_tok(C, i, to_c).start()
    wlocal(2).start()
    tok_local = pltpu.make_async_copy(tok_in, tok.at[mine], misc.at[3])
    tok_local.start()
    for n in (0, 1):
        got_pair(n)
        own_part(n, 1 - y)
    for i in range(PIECES):
        if not via_y(i):
            own_tok(Y, i, to_y).start()

    dec_local.start()
    dec_local.wait()
    remote(dec_in.at[y], dec.at[1 - y], misc.at[0], misc.at[1], to_y).wait_recv()
    lane = lax.broadcasted_iota(jnp.int32, (8, BLK), 1)
    for yy in range(2):
        run = dec[yy]
        step = 1
        while step < BLK:
            run = run + jnp.where(lane >= step, pltpu.roll(run, step, 1), 0.0)
            step *= 2
        dec[yy] = run
        cols[yy] = run.T
    for h in range(heads):
        for b in range(nb):
            at = h * nb + b

            def fading(yy, _, h=h, b=b, at=at):
                gap = cols[yy, :, at : at + 1] - dec[yy, at : at + 1, :]
                t = lax.broadcasted_iota(jnp.int32, (BLK, BLK), 0)
                u = lax.broadcasted_iota(jnp.int32, (BLK, BLK), 1)
                fade[h, yy * nb + b] = jnp.exp(jnp.where(t >= u, gap, -1e30))
                return 0

            lax.fori_loop(0, 2, fading, 0)

    def chunk(n, yy, r, at):
        p, lo, width = parts[n]
        w = wts[p, at, :, :, lo : lo + width].reshape(depth, width)
        ff, off = (at * depth) // kf, (at * depth) % kf
        if depth == kf:
            return dot(tok[yy * Fn + ff, r, :], w)
        if not isinstance(at, int):
            off = pl.multiple_of(off, HEAD)
        return dot(tok[yy * Fn + ff, r, pl.ds(off, depth)], w)

    def partial(n, yy, r):
        total = chunk(n, yy, r, near)
        for at in range(1, Z - 1):
            total = total + chunk(n, yy, r, at)
        return total

    def begin(n, i):
        r = slice(i * BLK, (i + 1) * BLK)
        kvacc[n, r, :] = partial(n, y, pl.ds(i * BLK, BLK))

    def finish(n, yy, i, total):
        total = total + chunk(n, yy, pl.ds(i * BLK, BLK), far)
        to = pl.ds(pl.multiple_of(yy * rows + i * BLK, BLK), BLK)
        if n == 0:
            keys[to, :] = silu(total).astype(BF16)
        else:
            vals[to, :] = total.astype(BF16)

    def project(n, yy, i):
        finish(n, yy, i, partial(n, yy, pl.ds(i * BLK, BLK)))

    def states(yy, b):
        j = yy * nb + b
        r = pl.ds(pl.multiple_of(j * BLK, BLK), BLK)
        for h in range(heads):
            hc = slice(h * HEAD, (h + 1) * HEAD)
            at = h * nb + b
            run = cols[yy, :, at : at + 1]
            end = dec[yy, at : at + 1, BLK - 1 : BLK]
            high, low = split(keys[r, hc].astype(F32) * jnp.exp(end - run))
            v = vals[r, hc]
            fresh[h, j] = dot(high, v, ((0,), (0,))) + dot(low, v, ((0,), (0,)))

    def got_core(kinds, i):
        lo, hi = i * PIECES // nb, (i + 1) * PIECES // nb
        for j in range(lo, hi):
            for kind in kinds:
                got_tok(kind, j)

    def begin_query():
        def tile(i, _):
            yy, b = i // nb, i % nb
            r = pl.ds(pl.multiple_of(b * BLK, BLK), BLK)
            qacc[pl.ds(pl.multiple_of(i * BLK, BLK), BLK), :] = partial(2, yy, r)
            return 0

        lax.fori_loop(0, 2 * nb, tile, 0)

    wsteps(0, 0)
    wsteps(1, 0)
    side_step(0)
    pair_step(0)
    own_tok(Y, PIECES - 1, to_y).start()
    wpair(2).start()
    for i in range(1, PIECES - 1):
        side_step(i)
        pair_step(i)
    side_step(PIECES - 1)
    wsteps(0, 1)
    wsteps(1, 1)
    pair_step(PIECES - 1)
    own_query(2)
    tok_local.wait()
    for i in range(nb):
        got_core((C, CX), i)
        begin(0, i)
        begin(1, i)
        if i == 0:
            diag_step(0)
    for i in range(1, PIECES // nb):
        diag_step(i)
    diag_step(PIECES - 1)
    wsteps(0, 2)
    wsteps(1, 2)
    for i in range(nb):
        finish(0, y, i, kvacc[0, i * BLK : (i + 1) * BLK, :])
        finish(1, y, i, kvacc[1, i * BLK : (i + 1) * BLK, :])
    got_core((CY, CD), 0)
    project(0, 1 - y, 0)
    project(1, 1 - y, 0)
    for i in range(PIECES // nb, PIECES - 1):
        diag_step(i)
    for b in range(nb):
        states(y, b)
    states(1 - y, 0)
    for i in range(1, nb):
        got_core((CY, CD), i)
        project(0, 1 - y, i)
        project(1, 1 - y, i)
        states(1 - y, i)

    def state_copy(to):
        return remote(
            s_out, s_in.at[z], ssend.at[to], srecv.at[z], (to * 2 + y, f)
        )

    def block_end(h, j):
        at = h * nb + j % nb
        return dec[j // nb, at : at + 1, BLK - 1 : BLK]

    for h in range(heads):
        state = jnp.zeros((HEAD, HEAD), F32)
        lead = jnp.zeros((1, 1), F32)
        for j in range(2 * nb):
            before[h, j] = state
            state = jnp.exp(block_end(h, j)) * state + fresh[h, j]
            lead = lead + block_end(h, j)
        s_out[h, 0:HEAD, :] = state.astype(BF16)
        high, low = split(jnp.broadcast_to(jnp.exp(lead), (8, HEAD)))
        s_out[h, HEAD : HEAD + 16, :] = jnp.concatenate([high, low], axis=0)
    for to in range(1, Z):

        @pl.when(to > z)
        def _(to=to):
            state_copy(to).start()

    got_near(2)
    begin_query()

    def place_out(b, who):
        return out.at[pl.ds(b * BLK, BLK), pl.ds(pl.multiple_of(who * half, HEAD), half)]

    def give(b):
        src = done.at[(1 - y) * nb + b]
        return remote(src, place_out(b, y), osend.at[b], orecv.at[b], to_y)

    def keep(b):
        return pltpu.make_async_copy(done.at[y * nb + b], place_out(b, y), oloc.at[b])

    def from_state(q, h, j, run):
        high, low = split(before[h, j])
        inter = dot(q, jnp.concatenate([high, low], axis=1))
        return jnp.exp(run) * (inter[:, :HEAD] + inter[:, HEAD:])

    def attend(yy, b):
        j = yy * nb + b
        r = pl.ds(pl.multiple_of(j * BLK, BLK), BLK)
        queries = silu(qacc[r, :] + chunk(2, yy, pl.ds(b * BLK, BLK), far)).astype(BF16)
        qry[r, :] = queries
        for h in range(heads):
            at = h * nb + b
            hc = slice(h * HEAD, (h + 1) * HEAD)
            q, k, v = queries[:, hc], keys[r, hc], vals[r, hc]
            scores = dot(q, k, ((1,), (1,)))
            weights = (fade[h, j] * scores).astype(BF16)
            qacc[r, hc] = dot(weights, v) + from_state(q, h, j, cols[yy, :, at : at + 1])

    def complete(yy, b):
        j = yy * nb + b
        r = pl.ds(pl.multiple_of(j * BLK, BLK), BLK)
        for h in range(heads):
            at = h * nb + b
            hc = slice(h * HEAD, (h + 1) * HEAD)
            mixed = qacc[r, hc] + from_state(qry[r, hc], h, j, cols[yy, :, at : at + 1])
            scale = lax.rsqrt(jnp.mean(mixed * mixed, axis=-1, keepdims=True) + 1e-6)
            done[j, :, hc] = (mixed * scale).astype(BF16)

    got_query(2, far)
    for b in range(nb):
        attend(1 - y, b)
    for b in range(nb):
        attend(y, b)

    enter[...] = jnp.zeros_like(enter)
    for at in range(Z - 1):

        @pl.when(at < z)
        def _(at=at):
            remote(s_out, s_in.at[at], ssend.at[at], srecv.at[at], (at * 2 + y, f)).wait_recv()
            for h in range(heads):
                terms = s_in[at, h, HEAD : HEAD + 16, :].astype(F32)
                decay = terms[0:1] + terms[8:9]
                enter[h] = decay * enter[h] + s_in[at, h, 0:HEAD, :].astype(F32)

    for h in range(heads):
        lead = jnp.zeros((1, 1), F32)
        for j in range(2 * nb):
            before[h, j] = jnp.exp(lead) * enter[h]
            lead = lead + block_end(h, j)

    for b in range(nb):
        complete(1 - y, b)
        give(b).start()
    for b in range(nb):
        complete(y, b)
        keep(b).start()

    for b in range(nb):
        keep(b).wait()
        give(b).wait_send()
        remote(
            done.at[y * nb + b], place_out(b, 1 - y), osend.at[b], orecv.at[b], to_y
        ).wait_recv()

    for to in range(1, Z):

        @pl.when(to > z)
        def _(to=to):
            state_copy(to).wait_send()

    dec_copy.wait_send()
    for n in range(len(parts)):
        wpair(n).wait_send()
    for at in range(Z):
        for n in range(2):
            for yy in range(2):

                @pl.when(has_r & (at <= z))
                def _(n=n, at=at, yy=yy):
                    wright(n, at, yy).wait_send()

                @pl.when(has_l & (at >= z))
                def _(n=n, at=at, yy=yy):
                    wleft(n, at, yy).wait_send()

        @pl.when(at != z)
        def _(at=at):
            for yy in range(2):
                wdirect(2, at, yy).wait_send()

    for i in range(PIECES):
        own_tok(X, i, to_x).wait_send()
        own_tok(Y, i, to_y).wait_send()
        own_tok(C, i, to_c).wait_send()
        tcopy(CX, i, to_c, place[X]).wait_send()
        tcopy(CY, i, to_c, place[Y]).wait_send()
        tcopy(CD, i, to_c, place[D]).wait_send()
        if via_y(i):
            tcopy(D, i, to_y, place[X]).wait_send()
        else:
            tcopy(D, i, to_x, place[Y]).wait_send()


def on_device(S, Fn, tokens, projection, log_decay):
    rows, kf = tokens.shape
    ks, width = projection.shape[1:]
    Z = S // 2
    half = width // 2
    heads = half // HEAD
    nb = rows // BLK
    parts = 3
    dec = log_decay.T.reshape(2, heads * nb, BLK)
    dec = jnp.pad(dec, ((0, 0), (0, 8 - heads * nb), (0, 0)))
    dma = pltpu.SemaphoreType.DMA
    any_spec = pl.BlockSpec(memory_space=pl.ANY)
    return pl.pallas_call(
        functools.partial(kernel, S, Fn),
        out_shape=jax.ShapeDtypeStruct((rows, width), BF16),
        in_specs=[any_spec] * 3,
        out_specs=any_spec,
        scratch_shapes=[
            pltpu.VMEM((2 * Fn, rows, kf), BF16),
            pltpu.VMEM((3, Z, 2, ks, half), BF16),
            pltpu.VMEM((2, 8, BLK), F32),
            pltpu.VMEM((2, BLK, 8), F32),
            pltpu.VMEM((heads, 2 * nb, BLK, BLK), F32),
            pltpu.VMEM((2 * rows, half), BF16),
            pltpu.VMEM((2 * rows, half), BF16),
            pltpu.VMEM((2 * rows, half), F32),
            pltpu.VMEM((2 * rows, half), BF16),
            pltpu.VMEM((heads, 2 * nb, HEAD, HEAD), F32),
            pltpu.VMEM((heads, 2 * nb, HEAD, HEAD), F32),
            pltpu.VMEM((2, rows, half), F32),
            pltpu.VMEM((heads, HEAD, HEAD), F32),
            pltpu.VMEM((Z, heads, HEAD + 16, HEAD), BF16),
            pltpu.VMEM((heads, HEAD + 16, HEAD), BF16),
            pltpu.VMEM((2 * nb, BLK, half), BF16),
            dma((7, PIECES)),
            dma((7, PIECES)),
            dma((parts,)),
            dma((parts,)),
            dma((parts,)),
            dma((parts, Z, 2)),
            dma((parts, Z, 2)),
            dma((parts, Z, 2)),
            dma((4,)),
            dma((Z,)),
            dma((Z,)),
            dma((nb,)),
            dma((nb,)),
            dma((nb,)),
        ],
        compiler_params=pltpu.CompilerParams(
            collective_id=0, has_side_effects=True, vmem_limit_bytes=52 * 1024 * 1024
        ),
    )(tokens, projection, dec)


def solution(mesh):
    S, Fn = mesh.shape["seq"], mesh.shape["fsdp"]
    return jax.shard_map(
        functools.partial(on_device, S, Fn),
        mesh=mesh,
        in_specs=(P("seq", "fsdp"), P(None, "seq", "fsdp"), P("seq", "fsdp")),
        out_specs=P("seq", "fsdp"),
        check_vma=False,
    )
```
